256 devices in a mesh: dp: 4 (over z_lo, core), fsdp: 64 (over x, z_hi, y).
Axes of the slice: x: 4, y: 4, z: 8 (z_hi: 4, z_lo: 2; z = z_hi * 2 + z_lo), core: 2. Of those that a mesh axis runs over, the one named last changes fastest.
Arguments:
- inputs: bfloat16 [256, 768, 4608], P(('dp', 'fsdp')), may hold values from -24 to 24
- cotangent: bfloat16 [256, 768, 1024], P(('dp', 'fsdp')), may hold values from -6 to 6
- response_mask: int32 [256, 768], P(('dp', 'fsdp')), may hold values from 0 to 1, as said below
- policy: float32 [4608, 1024], P('fsdp'), may hold values from -0.09375 to 0.09375
- anchor: float32 [4608, 1024], P('fsdp'), may hold values from -0.09375 to 0.09375
Outputs:
- gradient: float32 [4608, 1024], P('fsdp')
- anchor_next: float32 [4608, 1024], P('fsdp')
The draws below stay inside these ranges and needn't reach their ends.
Inputs may be any that keep to these rules, and one draw needn't show every extreme that they name: `response_mask`: each sequence is a prompt of 96 to 383 tokens, then a run of response tokens of length at least 768/4 (cut at the sequence's end), then padding.
All inputs are finite; a program needn't handle non-finite values.
Results may differ from the reference program's by a relative error of at most 0.0029.
Values may be sent and summed in bfloat16 or wider, within the bound.
A program may use at most 128 MiB of HBM per device.

```python
import jax
import jax.numpy as jnp
from jax import lax

D = 4608
KVW = 1024
LEN = 768
SEQS = 256


def draw_response_mask(key, part):
    key = jax.random.fold_in(key, 7)
    first_key, second_key = jax.random.split(key)
    prompt_end = jax.random.randint(first_key, (SEQS, 1), LEN // 8, LEN // 2)
    span = jax.random.randint(second_key, (SEQS, 1), LEN // 4, LEN + 1)
    finish = jnp.minimum(prompt_end + span, LEN)
    position = jnp.arange(LEN, dtype=jnp.int32)[None, :]
    return ((position >= prompt_end) & (position < finish)).astype(jnp.int32)


def raised(values, rng, source, target, parts, factor):
    def block_of(dim):
        return (jnp.arange(values.shape[dim]) // (values.shape[dim] // parts)).reshape((-1,) + (1,) * (values.ndim - 1 - dim))

    one_side = jax.random.permutation(rng, parts)[block_of(target)]
    second = (block_of(target) + parts // 2) % parts
    return jnp.where((block_of(source) == one_side) | (block_of(source) == second), factor * values, values)


def steps_of(stream_key, shape, shards, low, high):
    level, own = 1.0, jax.random.fold_in(stream_key, 6)
    for dim, blocks in shards:
        draws = jnp.exp(jax.random.uniform(jax.random.fold_in(own, dim), (blocks,), jnp.float32, low / len(shards), high / len(shards)))
        level = level * jnp.repeat(draws, shape[dim] // blocks).reshape([-1 if axis == dim else 1 for axis in range(len(shape))])
    return level


def centred(rng, shape, scale, reach, cuts=(), held_as=jnp.bfloat16):
    level = steps_of(rng, shape, cuts, -0.22, 0.18) if cuts else 1.0
    entries = jax.random.normal(rng, shape, jnp.float32) * scale * level
    return jnp.minimum(jnp.maximum(entries, -reach), reach).astype(held_as)


def gaussian_with(key, dims, scale, reach, cuts, heavy, kind=jnp.bfloat16):
    values = scale * jax.random.normal(key, dims, jnp.float32)
    if cuts:
        values = values * steps_of(key, dims, cuts, -0.22, 0.18)
    return jnp.clip(raised(values, jax.random.fold_in(key, 3), *heavy), -reach, reach).astype(kind)


def setup_inputs(seed: int = 0) -> dict:
    keys = jax.random.split(jax.random.key(seed), 6)
    inputs = gaussian_with(keys[0], (SEQS, LEN, D), 1.0, 24.0, ((0, 256),), (0, 2, 256, 6.0))
    cotangent = centred(keys[1], (SEQS, LEN, KVW), 1.0, 6.0, ((0, 256),))
    response_mask = draw_response_mask(jax.random.fold_in(keys[5], 71), 0)
    policy = centred(keys[3], (D, KVW), D ** -0.5, 0.09375, ((0, 64),), jnp.float32)
    anchor = centred(keys[4], (D, KVW), D ** -0.5, 0.09375, ((0, 64),), jnp.float32)
    return {"inputs": inputs, "cotangent": cotangent, "response_mask": response_mask, "policy": policy, "anchor": anchor}


kl_weight = 0.5
ema_rate = 0.01
step_size = 0.1


def reference(inputs, cotangent, response_mask, policy, anchor):
    tokens_flat = inputs.reshape(SEQS * LEN, D)
    delta = (policy - anchor).astype(jnp.bfloat16)
    spread = jnp.dot(tokens_flat, delta, preferred_element_type=jnp.float32).reshape(SEQS, LEN, KVW)
    weights_mask = response_mask.astype(jnp.float32)
    counted = jnp.sum(weights_mask, axis=1)
    signal = weights_mask[:, :, None] * (cotangent.astype(jnp.float32) + kl_weight * spread) / counted[:, None, None]
    signal = signal.astype(jnp.bfloat16).reshape(SEQS * LEN, KVW)
    gradient = lax.dot_general(tokens_flat, signal, (((0,), (0,)), ((), ())), preferred_element_type=jnp.float32)
    anchor_next = (1.0 - ema_rate) * anchor + ema_rate * (policy - step_size * gradient)
    return gradient, anchor_next
```

```python
import functools

import jax
import jax.numpy as jnp
from jax import lax
from jax.experimental import pallas as pl
from jax.experimental.pallas import tpu as pltpu
from jax.sharding import PartitionSpec as P

kl_weight = 0.5
ema_rate = 0.01
step_size = 0.1

MESH = pl.DeviceIdType.MESH
F32 = jnp.float32
BF16 = jnp.bfloat16

LEN = 768
D = 4608
KVW = 1024
HALF = KVW // 2
ROWS = 72
SLAB = 16 * ROWS
PACK = 2 * ROWS
ORDER = (2, 1, 3, 0)


def kernel(x_hbm, cot_hbm, mask_ref, policy_ref, anchor_ref, grad_ref, next_ref,
           xv, ta, tb, stage, dcol, spread, cot, sig_t, scale, gn, ga, gb, ra, rb,
           ha, hb, ha16, hb16, r2a, r2b, js, js16, zr, zsum, fin,
           loc, sib_s, sib_r, p1_s, p1_r, p2_s, p2_r, p3a_s, p3a_r, p3b_s, p3b_r,
           q1a_s, q1a_r, q1b_s, q1b_r, q2_s, q2_r, q3_s, q3_r, q4_s, q4_r):
    dp, fs = lax.axis_index("dp"), lax.axis_index("fsdp")
    c, zl = dp % 2, dp // 2
    x, zh, y = fs // 16, (fs // 4) % 4, fs % 4
    z = zh * 2 + zl

    def at(c_, x_, y_, z_):
        return ((z_ % 2) * 2 + c_, (x_ * 4 + z_ // 2) * 4 + y_)

    def on_x(k):
        return at(c, (x + k) % 4, y, z)

    def on_y(k):
        return at(c, x, (y + k) % 4, z)

    def on_z(k):
        return at(c, x, y, (z + k) % 8)

    sibling = at(1 - c, x, y, z)
    partner = at(c, x, y, zh * 2 + (1 - zl))
    diagonal = at(1 - c, x, y, zh * 2 + (1 - zl))

    sends = []

    def push(src, dst, ssem, rsem, device):
        copy = pltpu.make_async_remote_copy(
            src_ref=src, dst_ref=dst, send_sem=ssem, recv_sem=rsem,
            device_id=device, device_id_type=MESH)
        copy.start()
        sends.append(copy)
        return copy

    own_x = pltpu.make_async_copy(x_hbm.at[0], xv.at[pl.ds(0, LEN)], loc.at[0])
    own_x.start()
    mine = pl.multiple_of(c * HALF, HALF)
    other = pl.multiple_of((1 - c) * HALF, HALF)
    own_cot = pltpu.make_async_copy(
        cot_hbm.at[0, :, pl.ds(mine, HALF)], cot.at[pl.ds(0, LEN)], loc.at[1])
    own_cot.start()

    barrier = pltpu.get_barrier_semaphore()
    peers = [on_x(k) for k in (1, 2, 3)] + [on_y(k) for k in (1, 2, 3)]
    peers += [on_z(k) for k in range(1, 8)] + [sibling, diagonal]
    for device in peers:
        pl.semaphore_signal(barrier, inc=1, device_id=device, device_id_type=MESH)

    delta = policy_ref[...] - anchor_ref[...]
    delta = jnp.where(c == 0, delta[:, :HALF], delta[:, HALF:])
    blocks = [delta[:, 128 * i:128 * (i + 1)] for i in range(4)]
    ta[x, y, zh] = jnp.concatenate(blocks[:2], axis=0).astype(BF16)
    tb[y, x, zh] = jnp.concatenate(blocks[2:], axis=0).astype(BF16)
    weights = mask_ref[...].astype(F32)
    weights = weights / jnp.sum(weights, axis=1, keepdims=True)
    scale[0] = jnp.broadcast_to(weights, (8, LEN))

    pl.semaphore_wait(barrier, len(peers))

    p1 = []
    for k in (1, 2, 3):
        device = on_z(jnp.where(zl == 1, k, 8 - k))
        p1.append(push(ta.at[x, y, zh], ta.at[x, y, zh], p1_s.at[0, k - 1], p1_r.at[0, k - 1], device))
        p1.append(push(tb.at[y, x, zh], tb.at[y, x, zh], p1_s.at[1, k - 1], p1_r.at[1, k - 1], device))

    sib = [
        push(x_hbm.at[0], xv.at[pl.ds(LEN, LEN)], sib_s.at[0], sib_r.at[0], sibling),
        push(cot_hbm.at[0, :, pl.ds(other, HALF)], cot.at[pl.ds(LEN, LEN)], sib_s.at[1], sib_r.at[1], sibling),
        push(scale.at[0], scale.at[1], sib_s.at[2], sib_r.at[2], sibling),
    ]

    for copy in p1:
        copy.wait_recv()
    p2 = []
    for k in (1, 2, 3):
        p2.append(push(ta.at[x, y], ta.at[x, y], p2_s.at[0, k - 1], p2_r.at[0, k - 1], on_y(k)))
        p2.append(push(tb.at[y, x], tb.at[y, x], p2_s.at[1, k - 1], p2_r.at[1, k - 1], on_x(k)))

    spread[...] = jnp.zeros_like(spread)
    for copy in p2:
        copy.wait_recv()
    p3a, p3b = [], []
    for k in (1, 2, 3):
        p3a.append(push(ta.at[x], ta.at[x], p3a_s.at[k - 1], p3a_r.at[k - 1], on_x(k)))
    for j in range(4):
        xs = (x + j) % 4
        p3b.append([push(tb.at[y, xs], tb.at[y, xs], p3b_s.at[j, k - 1], p3b_r.at[j, k - 1], on_y(k))
                    for k in (1, 2, 3)])

    own_x.wait()
    own_cot.wait()
    for copy in sib:
        copy.wait_recv()

    def first_product(load, xs, part):
        def unpack(i, carry):
            v = load(i // 4, i % 4).astype(F32)
            row = pl.ds(pl.multiple_of((i % 4) * 288 + (i // 4) * ROWS, 8), ROWS)
            stage[row, 0:128] = v[:ROWS]
            stage[row, 128:256] = v[ROWS:]
            return carry
        lax.fori_loop(0, 16, unpack, 0)
        dcol[...] = stage[...].astype(BF16)

        def tokens(m, carry):
            rows = pl.ds(pl.multiple_of(m * 512, 512), 512)
            lhs = xv[rows, pl.ds(pl.multiple_of(xs * SLAB, 128), SLAB)]
            spread[rows, part * 256:(part + 1) * 256] += jnp.dot(lhs, dcol[...], preferred_element_type=F32)
            return carry
        lax.fori_loop(0, 3, tokens, 0)

    def product_a(xs):
        first_product(lambda yy, zz: ta[xs, yy, zz], xs, 0)

    def product_b(xs):
        first_product(lambda yy, zz: tb[yy, xs, zz], xs, 1)

    def ready_b(j):
        for copy in p3b[j]:
            copy.wait_recv()
        product_b((x + j) % 4)

    def ready_a(k):
        p3a[k - 1].wait_recv()
        product_a((x + 4 - k) % 4)

    product_a(x)
    ready_b(0)
    ready_b(1)
    ready_a(1)
    ready_a(3)
    ready_b(2)
    ready_a(2)
    ready_b(3)

    def make_signal(m, carry):
        rows = pl.ds(pl.multiple_of(m * 256, 256), 256)
        u = cot[rows, :].astype(F32) + kl_weight * spread[rows, :]
        lane = pl.ds(pl.multiple_of((m % 3) * 256, 256), 256)
        w = scale[m // 3, 0:1, lane]
        sig_t[:, rows] = (u.T * w).astype(BF16)
        return carry
    lax.fori_loop(0, 6, make_signal, 0)

    def natural(xs, yy, zz):
        return pl.ds(pl.multiple_of(xs * SLAB + zz * 288 + yy * ROWS, 8), ROWS)

    def own(rows, part):
        return jnp.concatenate([gn[rows, part * 256:part * 256 + 128],
                                gn[rows, part * 256 + 128:part * 256 + 256]], axis=0)

    q1a = [None] * 3
    q1b = [None] * 4
    for i, off in enumerate(ORDER):
        xs = (x + off) % 4
        out = jnp.dot(sig_t[...], xv[:, pl.ds(pl.multiple_of(xs * SLAB, 128), SLAB)],
                      preferred_element_type=F32)
        gn[pl.ds(pl.multiple_of(xs * SLAB, 8), SLAB), :] = out.T

        def pack_b(n, carry):
            yy, zz = (y + 1 + n // 4) % 4, n % 4
            gb[yy, xs, zz] = own(natural(xs, yy, zz), 1).astype(BF16)
            return carry
        lax.fori_loop(0, 12, pack_b, 0)
        q1b[i] = [push(gb.at[(y + k) % 4, xs], rb.at[k - 1, xs], q1b_s.at[i, k - 1], q1b_r.at[i, k - 1], on_y(k))
                  for k in (2, 1, 3)]
        if off:
            def pack_a(n, carry):
                yy, zz = n // 4, n % 4
                ga[xs, yy, zz] = own(natural(xs, yy, zz), 0).astype(BF16)
                return carry
            lax.fori_loop(0, 16, pack_a, 0)
            q1a[off - 1] = push(ga.at[xs], ra.at[off - 1], q1a_s.at[off - 1], q1a_r.at[off - 1], on_x(off))

    q2 = []
    for i, off in enumerate(ORDER):
        xs = (x + off) % 4
        for copy in q1b[i]:
            copy.wait_recv()

        def sum_b(zz, carry):
            t = own(natural(xs, y, zz), 1)
            for k in range(3):
                t = t + rb[k, xs, zz].astype(F32)
            hb[xs, zz] = t
            hb16[xs, zz] = t.astype(BF16)
            return carry
        lax.fori_loop(0, 4, sum_b, 0)
        if off:
            q2.append(push(hb16.at[xs], r2b.at[off - 1], q2_s.at[1, off - 1], q2_r.at[1, off - 1], on_x(off)))

    for copy in q1a:
        copy.wait_recv()
    for off in ORDER:
        yy = (y + off) % 4

        def sum_a(zz, carry):
            t = own(natural(x, yy, zz), 0)
            for k in range(3):
                t = t + ra[k, yy, zz].astype(F32)
            ha[yy, zz] = t
            ha16[yy, zz] = t.astype(BF16)
            return carry
        lax.fori_loop(0, 4, sum_a, 0)
        if off:
            q2.append(push(ha16.at[yy], r2a.at[off - 1], q2_s.at[0, off - 1], q2_r.at[0, off - 1], on_y(off)))

    for copy in q2:
        copy.wait_recv()

    def sum_2(zz, carry):
        a, b = ha[y, zz], hb[x, zz]
        for k in range(3):
            a = a + r2a[k, zz].astype(F32)
            b = b + r2b[k, zz].astype(F32)
        js[zz, 0] = a
        js[zz, 1] = b
        js16[zz, 0] = a.astype(BF16)
        js16[zz, 1] = b.astype(BF16)
        return carry
    lax.fori_loop(0, 4, sum_2, 0)

    q3 = []
    for k in (4, 3, 5, 2, 6, 1, 7):
        there = (z + k) % 8
        window = pl.ds(pl.multiple_of((there % 2) * 64, 16), 80)
        q3.append(push(js16.at[there // 2, :, window], zr.at[k - 1], q3_s.at[k - 1], q3_r.at[k - 1], on_z(k)))
    for copy in q3:
        copy.wait_recv()
    total = js[zh, :, pl.ds(pl.multiple_of(zl * 64, 8), 80), :]
    for k in range(7):
        total = total + zr[k].astype(F32)
    zsum[...] = total
    fin[c, zl] = zsum[:, pl.ds(pl.multiple_of(zl * 8, 8), ROWS), :]

    q4 = [push(fin.at[c, zl], fin.at[c, zl], q4_s.at[n], q4_r.at[n], device)
          for n, device in enumerate((diagonal, partner, sibling))]
    for copy in q4:
        copy.wait_recv()

    for i in range(8):
        cols = slice(128 * i, 128 * (i + 1))
        g = fin[i // 4, i % 2, (i // 2) % 2]
        grad_ref[:, cols] = g
        next_ref[:, cols] = (1.0 - ema_rate) * anchor_ref[:, cols] + ema_rate * (
            policy_ref[:, cols] - step_size * g)

    for copy in sends:
        copy.wait_send()


def shards(inputs, cotangent, response_mask, policy, anchor):
    vmem = pl.BlockSpec(memory_space=pltpu.VMEM)
    hbm = pl.BlockSpec(memory_space=pl.ANY)
    dma = pltpu.SemaphoreType.DMA
    packed = (PACK, 128)
    scratch = [
        pltpu.VMEM((2 * LEN, D), BF16),
        pltpu.VMEM((4, 4, 4) + packed, BF16),
        pltpu.VMEM((4, 4, 4) + packed, BF16),
        pltpu.VMEM((SLAB, 256), F32),
        pltpu.VMEM((SLAB, 256), BF16),
        pltpu.VMEM((2 * LEN, HALF), F32),
        pltpu.VMEM((2 * LEN, HALF), BF16),
        pltpu.VMEM((HALF, 2 * LEN), BF16),
        pltpu.VMEM((2, 8, LEN), F32),
        pltpu.VMEM((D, HALF), F32),
        pltpu.VMEM((4, 4, 4) + packed, BF16),
        pltpu.VMEM((4, 4, 4) + packed, BF16),
        pltpu.VMEM((3, 4, 4) + packed, BF16),
        pltpu.VMEM((3, 4, 4) + packed, BF16),
        pltpu.VMEM((4, 4) + packed, F32),
        pltpu.VMEM((4, 4) + packed, F32),
        pltpu.VMEM((4, 4) + packed, BF16),
        pltpu.VMEM((4, 4) + packed, BF16),
        pltpu.VMEM((3, 4) + packed, BF16),
        pltpu.VMEM((3, 4) + packed, BF16),
        pltpu.VMEM((4, 2) + packed, F32),
        pltpu.VMEM((4, 2) + packed, BF16),
        pltpu.VMEM((7, 2, 80, 128), BF16),
        pltpu.VMEM((2, 80, 128), F32),
        pltpu.VMEM((2, 2, 2, ROWS, 128), F32),
        dma((2,)), dma((3,)), dma((3,)),
        dma((2, 3)), dma((2, 3)), dma((2, 3)), dma((2, 3)),
        dma((3,)), dma((3,)), dma((4, 3)), dma((4, 3)),
        dma((3,)), dma((3,)), dma((4, 3)), dma((4, 3)),
        dma((2, 3)), dma((2, 3)), dma((7,)), dma((7,)), dma((3,)), dma((3,)),
    ]
    return pl.pallas_call(
        kernel,
        out_shape=(jax.ShapeDtypeStruct((ROWS, KVW), F32), jax.ShapeDtypeStruct((ROWS, KVW), F32)),
        in_specs=[hbm, hbm, vmem, vmem, vmem],
        out_specs=(vmem, vmem),
        scratch_shapes=scratch,
        compiler_params=pltpu.CompilerParams(
            collective_id=0, has_side_effects=True, vmem_limit_bytes=62 * 2**20),
        cost_estimate=pl.CostEstimate(flops=4 * LEN * D * KVW, bytes_accessed=20 * 2**20, transcendentals=0),
        name="policy_step",
    )(inputs, cotangent, response_mask, policy, anchor)


def solution(mesh):
    placed = (
        P(("dp", "fsdp"), None, None),
        P(("dp", "fsdp"), None, None),
        P(("dp", "fsdp"), None),
        P("fsdp", None),
        P("fsdp", None),
    )
    return jax.shard_map(
        shards,
        mesh=mesh,
        in_specs=placed,
        out_specs=(P("fsdp", None), P("fsdp", None)),
        check_vma=False,
    )
```

```python
import jax
import jax.numpy as jnp
from jax import lax
from jax.experimental import pallas as pl
from jax.experimental.pallas import tpu as pltpu
from jax.sharding import PartitionSpec as P

kl_weight = 0.5
ema_rate = 0.01
step_size = 0.1

MESH = pl.DeviceIdType.MESH
F32 = jnp.float32
BF16 = jnp.bfloat16

LEN = 768
D = 4608
KVW = 1024
HALF = KVW // 2
WIDE = HALF // 2
ROWS = 72
SLAB = 16 * ROWS
PACK = 2 * ROWS
ORDER = (2, 1, 3, 0)
CUTS = ((64, 48, 32), (48, 64, 32))
NSEM = 200


def kernel(x_hbm, cot_hbm, mask_ref, policy_ref, anchor_ref, grad_ref, next_ref,
           xv, stage, dcol, spread, cot, sig_t, scale, g32, fin, *rest):
    lanes = [rest[17 * i:17 * (i + 1)] for i in range(2)]
    ssem, rsem, loc = rest[34:]
    dp, fs = lax.axis_index("dp"), lax.axis_index("fsdp")
    c, zl = dp % 2, dp // 2
    x, zh, y = fs // 16, (fs // 4) % 4, fs % 4
    z = zh * 2 + zl

    def at(c_, x_, y_, z_):
        return ((z_ % 2) * 2 + c_, (x_ * 4 + z_ // 2) * 4 + y_)

    def on_x(k):
        return at(c, (x + k) % 4, y, z)

    def on_y(k):
        return at(c, x, (y + k) % 4, z)

    def on_z(k):
        return at(c, x, y, (z + k) % 8)

    def on_pairs(k):
        return on_z(jnp.where(zl == 1, k, 8 - k))

    sibling = at(1 - c, x, y, z)
    partner = at(c, x, y, zh * 2 + (1 - zl))
    diagonal = at(1 - c, x, y, zh * 2 + (1 - zl))

    sends = []

    def push(src, dst, device):
        n = len(sends)
        copy = pltpu.make_async_remote_copy(
            src_ref=src, dst_ref=dst, send_sem=ssem.at[n], recv_sem=rsem.at[n],
            device_id=device, device_id_type=MESH)
        copy.start()
        sends.append(copy)
        return copy

    def arrive(copies):
        for copy in copies:
            copy.wait_recv()

    own_x = pltpu.make_async_copy(x_hbm.at[0], xv.at[pl.ds(0, LEN)], loc.at[0])
    own_x.start()
    mine = pl.multiple_of(c * HALF, HALF)
    other = pl.multiple_of((1 - c) * HALF, HALF)
    own_cot = pltpu.make_async_copy(
        cot_hbm.at[0, :, pl.ds(mine, HALF)], cot.at[pl.ds(0, LEN)], loc.at[1])
    own_cot.start()

    barrier = pltpu.get_barrier_semaphore()
    peers = [on_x(k) for k in (1, 2, 3)] + [on_y(k) for k in (1, 2, 3)]
    peers += [on_z(k) for k in range(1, 8)] + [sibling, diagonal]
    for device in peers:
        pl.semaphore_signal(barrier, inc=1, device_id=device, device_id_type=MESH)

    delta = policy_ref[...] - anchor_ref[...]
    delta = jnp.where(c == 0, delta[:, :HALF], delta[:, HALF:])
    for n, (ta, tb, tc, *_) in enumerate(lanes):
        i, j, _ = CUTS[n]
        v = jnp.concatenate([delta[:, WIDE * n:WIDE * n + 128], delta[:, WIDE * n + 128:WIDE * n + 256]], axis=0)
        ta[x, y, zh] = v[:i].astype(BF16)
        tb[y, x, zh] = v[i:i + j].astype(BF16)
        tc[zh, x, y] = v[i + j:].astype(BF16)
    weights = mask_ref[...].astype(F32)
    weights = weights / jnp.sum(weights, axis=1, keepdims=True)
    scale[0] = jnp.broadcast_to(weights, (8, LEN))

    pl.semaphore_wait(barrier, len(peers))

    first = []
    for ta, tb, tc, *_ in lanes:
        first.append([
            [push(t, t, on_pairs(k)) for k in (1, 2, 3) for t in (ta.at[x, y, zh],)],
            [push(t, t, on_pairs(k)) for k in (1, 2, 3) for t in (tb.at[y, x, zh],)],
            [push(t, t, on_y(k)) for k in (1, 2, 3) for t in (tc.at[zh, x, y],)]])

    sib = [
        push(x_hbm.at[0], xv.at[pl.ds(LEN, LEN)], sibling),
        push(cot_hbm.at[0, :, pl.ds(other, HALF)], cot.at[pl.ds(LEN, LEN)], sibling),
        push(scale.at[0], scale.at[1], sibling),
    ]

    second = []
    for n, (ta, tb, tc, *_) in enumerate(lanes):
        arrive(first[n][0])
        pa = [push(ta.at[x, y], ta.at[x, y], on_y(k)) for k in (1, 2, 3)]
        arrive(first[n][1])
        pb = [push(tb.at[y, x], tb.at[y, x], on_x(k)) for k in (1, 2, 3)]
        arrive(first[n][2])
        pc = [push(tc.at[zh, x], tc.at[zh, x], on_x(k)) for k in (1, 2, 3)]
        second.append([pa, pb, pc])

    third = []
    for n, (ta, tb, tc, *_) in enumerate(lanes):
        slabs = [[], [], [], []]
        arrive(second[n][0])
        for k in (3, 2, 1):
            slabs[4 - k].append(push(ta.at[x], ta.at[x], on_x(k)))
        arrive(second[n][1])
        arrive(second[n][2])
        for j in range(4):
            xs = (x + j) % 4
            for k in (1, 2, 3):
                slabs[j].append(push(tb.at[y, xs], tb.at[y, xs], on_y(k)))
            for k in (1, 2, 3):
                slabs[j].append(push(tc.at[zh, xs], tc.at[zh, xs], on_pairs(k)))
        third.append(slabs)

    own_x.wait()
    own_cot.wait()
    arrive(sib)

    def first_product(n, j):
        ta, tb, tc = lanes[n][:3]
        xs = (x + j) % 4
        arrive(third[n][j])

        def unpack(i, carry):
            yy, zz = i // 4, i % 4
            v = jnp.concatenate([ta[xs, yy, zz].astype(F32), tb[yy, xs, zz].astype(F32),
                                 tc[zz, xs, yy].astype(F32)], axis=0)
            row = pl.ds(pl.multiple_of(zz * 288 + yy * ROWS, 8), ROWS)
            stage[row, 0:128] = v[:ROWS]
            stage[row, 128:256] = v[ROWS:]
            return carry
        lax.fori_loop(0, 16, unpack, 0)
        dcol[...] = stage[...].astype(BF16)

        def tokens(m, carry):
            rows = pl.ds(pl.multiple_of(m * 512, 512), 512)
            lhs = xv[rows, pl.ds(pl.multiple_of(xs * SLAB, 128), SLAB)]
            out = jnp.dot(lhs, dcol[...], preferred_element_type=F32)
            spread[rows, :] = out if j == 0 else spread[rows, :] + out
            return carry
        lax.fori_loop(0, 3, tokens, 0)

    def make_signal(n):
        cols = slice(WIDE * n, WIDE * (n + 1))

        def tokens(m, carry):
            rows = pl.ds(pl.multiple_of(m * 256, 256), 256)
            u = cot[rows, cols].astype(F32) + kl_weight * spread[rows, :]
            lane = pl.ds(pl.multiple_of((m % 3) * 256, 256), 256)
            w = scale[m // 3, 0:1, lane]
            sig_t[cols, rows] = (u.T * w).astype(BF16)
            return carry
        lax.fori_loop(0, 6, tokens, 0)

    heavy = [([], [[], [], [], []], []), ([], [[], [], [], []], [])]

    def second_product(n, i):
        ga, gb, gc, ra, rb, rc = lanes[n][3:9]
        p, q, _ = CUTS[n]
        off = ORDER[i]
        xs = (x + off) % 4
        out = jnp.dot(sig_t[WIDE * n:WIDE * (n + 1), :], xv[:, pl.ds(pl.multiple_of(xs * SLAB, 128), SLAB)],
                      preferred_element_type=F32)
        stage[...] = out.T

        def pack(m, carry):
            yy, zz = m // 4, m % 4
            row = pl.ds(pl.multiple_of(zz * 288 + yy * ROWS, 8), ROWS)
            v = jnp.concatenate([stage[row, 0:128], stage[row, 128:256]], axis=0)
            g32[n, xs, zz, yy] = v
            ga[xs, yy, zz] = v[:p].astype(BF16)
            gb[yy, xs, zz] = v[p:p + q].astype(BF16)
            gc[zz, xs, yy] = v[p + q:].astype(BF16)
            return carry
        lax.fori_loop(0, 16, pack, 0)
        if off:
            heavy[n][0].append(push(ga.at[xs], ra.at[off - 1], on_x(off)))
        for k in (2, 1, 3):
            heavy[n][1][i].append(push(gb.at[(y + k) % 4, xs], rb.at[k - 1, xs], on_y(k)))
        if i == 3:
            for k in (4, 3, 5, 2, 6, 1, 7):
                there = (z + k) % 8
                window = pl.ds(pl.multiple_of((there % 2) * 16, 16), 16)
                heavy[n][2].append(push(gc.at[there // 2, :, :, window], rc.at[k - 1], on_z(k)))

    middle = [([], [], []), ([], [], [])]

    def first_sums(n):
        ra, rb, rc, ha, hb, hc, r2a, r2b, r2c = lanes[n][6:15]
        ha, ha16 = ha
        hb, hb16 = hb
        hc, hc16 = hc
        p, q, _ = CUTS[n]
        for i, off in enumerate(ORDER):
            xs = (x + off) % 4
            arrive(heavy[n][1][i])

            def sum_b(zz, carry):
                t = g32[n, xs, zz, y, p:p + q, :]
                for k in range(3):
                    t = t + rb[k, xs, zz].astype(F32)
                hb[xs, zz] = t
                hb16[xs, zz] = t.astype(BF16)
                return carry
            lax.fori_loop(0, 4, sum_b, 0)
            if off:
                middle[n][1].append(push(hb16.at[xs], r2b.at[off - 1], on_x(off)))
        arrive(heavy[n][0])
        for off in ORDER:
            yy = (y + off) % 4

            def sum_a(zz, carry):
                t = g32[n, x, zz, yy, :p, :]
                for k in range(3):
                    t = t + ra[k, yy, zz].astype(F32)
                ha[yy, zz] = t
                ha16[yy, zz] = t.astype(BF16)
                return carry
            lax.fori_loop(0, 4, sum_a, 0)
            if off:
                middle[n][0].append(push(ha16.at[yy], r2a.at[off - 1], on_y(off)))
        arrive(heavy[n][2])
        for off in ORDER:
            xs = (x + off) % 4

            def sum_c(yy, carry):
                t = g32[n, xs, zh, yy, pl.ds(pl.multiple_of(p + q + zl * 16, 8), 16), :]
                for k in range(7):
                    t = t + rc[k, xs, yy].astype(F32)
                hc[xs, yy] = t
                hc16[xs, yy] = t.astype(BF16)
                return carry
            lax.fori_loop(0, 4, sum_c, 0)
            if off:
                middle[n][2].append(push(hc16.at[xs], r2c.at[off - 1], on_x(off)))

    last = [([], []), ([], [])]

    def second_sums(n):
        (ha, _), (hb, _), (hc, _), r2a, r2b, r2c, (js, jc), (r3, r3c) = lanes[n][9:17]
        js, js16 = js
        jc, jc16 = jc
        p, q, _ = CUTS[n]
        for copies in middle[n]:
            arrive(copies)

        def sum_ab(zz, carry):
            a, b = ha[y, zz], hb[x, zz]
            for k in range(3):
                a = a + r2a[k, zz].astype(F32)
                b = b + r2b[k, zz].astype(F32)
            for side in range(2):
                s, t = (p - 32) * side, (q - 32) * side
                v = jnp.concatenate([a[s:s + 32], b[t:t + 32]], axis=0)
                js[zz, side] = v
                js16[zz, side] = v.astype(BF16)
            return carry
        lax.fori_loop(0, 4, sum_ab, 0)
        for k in (4, 3, 5, 2, 6, 1, 7):
            there = (z + k) % 8
            last[n][0].append(push(js16.at[there // 2, there % 2], r3.at[k - 1], on_z(k)))
        for yy in range(4):
            t = hc[x, yy]
            for k in range(3):
                t = t + r2c[k, yy].astype(F32)
            jc[yy] = t
            jc16[yy] = t.astype(BF16)
        for k in (2, 1, 3):
            last[n][1].append(push(jc16.at[(y + k) % 4], r3c.at[k - 1], on_y(k)))

    done = [[], []]

    def last_sums(n):
        (js, jc), (r3, r3c) = lanes[n][15:17]
        arrive(last[n][0])
        t = js[0][zh, zl]
        for k in range(7):
            t = t + r3[k].astype(F32)
        arrive(last[n][1])
        u = jc[0][y]
        for k in range(3):
            u = u + r3c[k].astype(F32)
        fin[c, zl, n] = jnp.concatenate([t, u], axis=0)
        piece = fin.at[c, zl, n]
        done[n] += [push(piece, piece, device) for device in (diagonal, partner, sibling)]

    def finish(n):
        arrive(done[n])
        p, q, _ = CUTS[n]
        for core in range(2):
            lo, hi = fin[core, 0, n], fin[core, 1, n]
            v = jnp.concatenate([lo[0:32], hi[64 - p + 32 - 32:32], lo[32:64], hi[64 - q + 32:64],
                                 lo[64:80], hi[64:80]], axis=0)
            for half in range(2):
                begin = core * HALF + n * WIDE + half * 128
                cols = slice(begin, begin + 128)
                g = v[ROWS * half:ROWS * (half + 1)]
                grad_ref[:, cols] = g
                next_ref[:, cols] = (1.0 - ema_rate) * anchor_ref[:, cols] + ema_rate * (
                    policy_ref[:, cols] - step_size * g)

    for j in range(4):
        first_product(0, j)
    make_signal(0)
    for i in range(4):
        second_product(0, i)
    for j in range(4):
        first_product(1, j)
    make_signal(1)
    for i in range(3):
        second_product(1, i)
    first_sums(0)
    second_product(1, 3)
    second_sums(0)
    first_sums(1)
    last_sums(0)
    second_sums(1)
    finish(0)
    last_sums(1)
    finish(1)

    for copy in sends:
        copy.wait_send()


def shards(inputs, cotangent, response_mask, policy, anchor):
    vmem = pl.BlockSpec(memory_space=pltpu.VMEM)
    hbm = pl.BlockSpec(memory_space=pl.ANY)
    scratch = [
        pltpu.VMEM((2 * LEN, D), BF16),
        pltpu.VMEM((SLAB, WIDE), F32),
        pltpu.VMEM((SLAB, WIDE), BF16),
        pltpu.VMEM((2 * LEN, WIDE), F32),
        pltpu.VMEM((2 * LEN, HALF), BF16),
        pltpu.VMEM((HALF, 2 * LEN), BF16),
        pltpu.VMEM((2, 8, LEN), F32),
        pltpu.VMEM((2, 4, 4, 4, PACK, 128), F32),
        pltpu.VMEM((2, 2, 2, 80, 128), F32),
    ]
    for p, q, r in CUTS:
        scratch += [pltpu.VMEM((4, 4, 4, m, 128), BF16) for m in (p, q, r)]
        scratch += [pltpu.VMEM((4, 4, 4, m, 128), BF16) for m in (p, q, r)]
        scratch += [pltpu.VMEM((3, 4, 4, m, 128), BF16) for m in (p, q)]
        scratch += [pltpu.VMEM((7, 4, 4, 16, 128), BF16)]
        scratch += [(pltpu.VMEM((4, 4, m, 128), F32), pltpu.VMEM((4, 4, m, 128), BF16))
                    for m in (p, q, 16)]
        scratch += [pltpu.VMEM((3, 4, m, 128), BF16) for m in (p, q, 16)]
        scratch += [((pltpu.VMEM((4, 2, 64, 128), F32), pltpu.VMEM((4, 2, 64, 128), BF16)),
                     (pltpu.VMEM((4, 16, 128), F32), pltpu.VMEM((4, 16, 128), BF16)))]
        scratch += [(pltpu.VMEM((7, 64, 128), BF16), pltpu.VMEM((3, 16, 128), BF16))]
    scratch += [pltpu.SemaphoreType.DMA((NSEM,)), pltpu.SemaphoreType.DMA((NSEM,)),
                pltpu.SemaphoreType.DMA((2,))]
    return pl.pallas_call(
        kernel,
        out_shape=(jax.ShapeDtypeStruct((ROWS, KVW), F32), jax.ShapeDtypeStruct((ROWS, KVW), F32)),
        in_specs=[hbm, hbm, vmem, vmem, vmem],
        out_specs=(vmem, vmem),
        scratch_shapes=scratch,
        compiler_params=pltpu.CompilerParams(
            collective_id=0, has_side_effects=True, vmem_limit_bytes=62 * 2**20),
        cost_estimate=pl.CostEstimate(flops=4 * LEN * D * KVW, bytes_accessed=20 * 2**20, transcendentals=0),
        name="policy_step",
    )(inputs, cotangent, response_mask, policy, anchor)


def solution(mesh):
    placed = (
        P(("dp", "fsdp"), None, None),
        P(("dp", "fsdp"), None, None),
        P(("dp", "fsdp"), None),
        P("fsdp", None),
        P("fsdp", None),
    )
    return jax.shard_map(
        shards,
        mesh=mesh,
        in_specs=placed,
        out_specs=(P("fsdp", None), P("fsdp", None)),
        check_vma=False,
    )
```

```python
import jax
import jax.numpy as jnp
from jax import lax
from jax.experimental import pallas as pl
from jax.experimental.pallas import tpu as pltpu
from jax.sharding import PartitionSpec as P

kl_weight = 0.5
ema_rate = 0.01
step_size = 0.1

MESH = pl.DeviceIdType.MESH
F32 = jnp.float32
BF16 = jnp.bfloat16

LEN = 768
D = 4608
KVW = 1024
HALF = KVW // 2
WIDE = HALF // 2
ROWS = 72
SLAB = 16 * ROWS
PACK = 2 * ROWS
CUTS = ((64, 48, 32), (48, 64, 32))
NSEM = 61


def kernel(x_hbm, cot_hbm, mask_ref, policy_ref, anchor_ref, grad_ref, next_ref,
           xv, stage, dcol, spread, cot, sig_t, scale, g32, fin, *rest):
    lanes = [rest[17 * i:17 * (i + 1)] for i in range(2)]
    ssem, rsem, loc = rest[34:]
    dp, fs = lax.axis_index("dp"), lax.axis_index("fsdp")
    c, zl = dp % 2, dp // 2
    x, zh, y = fs // 16, (fs // 4) % 4, fs % 4
    z = zh * 2 + zl

    def at(c_, x_, y_, z_):
        return ((z_ % 2) * 2 + c_, (x_ * 4 + z_ // 2) * 4 + y_)

    def on_x(k):
        return at(c, (x + k) % 4, y, z)

    def on_y(k):
        return at(c, x, (y + k) % 4, z)

    def on_z(k):
        return at(c, x, y, (z + k) % 8)

    def on_pairs(k):
        return on_z(jnp.where(zl == 1, k, 8 - k))

    sibling = at(1 - c, x, y, z)
    partner = at(c, x, y, zh * 2 + (1 - zl))
    diagonal = at(1 - c, x, y, zh * 2 + (1 - zl))

    groups = []

    class Group:
        def __init__(self, span):
            self.span, self.n = span, len(groups)
            groups.append(self)

        def push(self, src, dst, device):
            pltpu.make_async_remote_copy(
                src_ref=src, dst_ref=dst, send_sem=ssem.at[self.n], recv_sem=rsem.at[self.n],
                device_id=device, device_id_type=MESH).start()

        def arrive(self):
            pltpu.make_async_copy(self.span, self.span, rsem.at[self.n]).wait()

        def sent(self):
            pltpu.make_async_copy(self.span, self.span, ssem.at[self.n]).wait()

    def spread_out(span, ref, targets):
        group = Group(span)
        for device in targets:
            group.push(ref, ref, device)
        return group

    def planar(n, xs, yy):
        return (yy, xs) if n else (xs, yy)

    on_slow, on_fast = (on_x, on_y), (on_y, on_x)

    own_x = pltpu.make_async_copy(x_hbm.at[0], xv.at[pl.ds(0, LEN)], loc.at[0])
    own_x.start()
    mine = pl.multiple_of(c * HALF, HALF)
    other = pl.multiple_of((1 - c) * HALF, HALF)
    own_cot = pltpu.make_async_copy(
        cot_hbm.at[0, :, pl.ds(mine, HALF)], cot.at[pl.ds(0, LEN)], loc.at[1])
    own_cot.start()

    barrier = pltpu.get_barrier_semaphore()
    peers = [on_x(k) for k in (1, 2, 3)] + [on_y(k) for k in (1, 2, 3)]
    peers += [on_z(k) for k in range(1, 8)] + [sibling, diagonal]
    for device in peers:
        pl.semaphore_signal(barrier, inc=1, device_id=device, device_id_type=MESH)

    delta = policy_ref[...] - anchor_ref[...]
    delta = jnp.where(c == 0, delta[:, :HALF], delta[:, HALF:])
    for n, (ta, tb, tc, *_) in enumerate(lanes):
        p, q, _ = CUTS[n]
        v = jnp.concatenate([delta[:, WIDE * n:WIDE * n + 128], delta[:, WIDE * n + 128:WIDE * n + 256]], axis=0)
        ta[x, y, zh] = v[:p].astype(BF16)
        tb[y, x, zh] = v[p:p + q].astype(BF16)
        tc[(zh, *planar(n, x, y))] = v[p + q:].astype(BF16)
    weights = mask_ref[...].astype(F32)
    weights = weights / jnp.sum(weights, axis=1, keepdims=True)
    scale[0] = jnp.broadcast_to(weights, (8, LEN))

    pl.semaphore_wait(barrier, len(peers))

    three = pl.ds(0, 3)
    first = []
    for n, (ta, tb, tc, *_) in enumerate(lanes):
        first.append([
            spread_out(ta.at[0, 0, three], ta.at[x, y, zh], [on_pairs(k) for k in (1, 2, 3)]),
            spread_out(tb.at[0, 0, three], tb.at[y, x, zh], [on_pairs(k) for k in (1, 2, 3)]),
            spread_out(tc.at[0, 0, three], tc.at[(zh, *planar(n, x, y))],
                       [on_fast[n](k) for k in (1, 2, 3)])])

    sib = [Group(xv.at[pl.ds(LEN, LEN)]), Group(cot.at[pl.ds(LEN, LEN)]), Group(scale.at[1])]
    sib[0].push(x_hbm.at[0], xv.at[pl.ds(LEN, LEN)], sibling)
    sib[1].push(cot_hbm.at[0, :, pl.ds(other, HALF)], cot.at[pl.ds(LEN, LEN)], sibling)
    sib[2].push(scale.at[0], scale.at[1], sibling)

    second = []
    for n, (ta, tb, tc, *_) in enumerate(lanes):
        first[n][0].arrive()
        pa = spread_out(ta.at[0, three], ta.at[x, y], [on_y(k) for k in (1, 2, 3)])
        first[n][1].arrive()
        pb = spread_out(tb.at[0, three], tb.at[y, x], [on_x(k) for k in (1, 2, 3)])
        first[n][2].arrive()
        pc = spread_out(tc.at[0, three], tc.at[zh, planar(n, x, y)[0]], [on_slow[n](k) for k in (1, 2, 3)])
        second.append([pa, pb, pc])

    front, back = pl.ds(0, 2), pl.ds(2, 2)

    def ring_start(t, me, on):
        one, two = Group(t.at[0]), Group(t.at[0])
        for group, rows, k in ((one, front, 1), (one, back, 3), (two, back, 1), (two, front, 3)):
            group.push(t.at[me, rows], t.at[me, rows], on(k))
        return one, two

    def ring_forward(t, me, on, started):
        started[0].arrive()
        group = Group(t.at[0])
        for owner, rows, k in (((me + 3) % 4, front, 1), ((me + 1) % 4, back, 3)):
            group.push(t.at[owner, rows], t.at[owner, rows], on(k))
        return started[1], group

    def third_start(n):
        ta, tb, tc = lanes[n][:3]
        second[n][0].arrive()
        a = ring_start(ta, x, on_x)
        second[n][1].arrive()
        b = ring_start(tb, y, on_y)
        second[n][2].arrive()
        c1 = [spread_out(tc.at[0, half], tc.at[zh, half], [on_pairs(1)]) for half in (front, back)]
        return a, b, c1

    def third_forward(n, started):
        ta, tb, tc = lanes[n][:3]
        a, b, c1 = started
        a = ring_forward(ta, x, on_x, a)
        b = ring_forward(tb, y, on_y, b)
        relay = Group(tc.at[pl.ds(0, 2)])
        owner = (zh + jnp.where(zl == 1, 1, 3)) % 4
        for group, half in zip(c1, (front, back)):
            group.arrive()
            for k in (1, 2):
                relay.push(tc.at[owner, half], tc.at[owner, half], on_z(jnp.where(zl == 1, 8 - k, k)))
        return (*a, *b, relay)

    def first_product(n):
        ta, tb, tc = lanes[n][:3]
        for xs in range(4):
            def unpack(i, carry):
                yy, zz = i // 4, i % 4
                v = jnp.concatenate([ta[xs, yy, zz].astype(F32), tb[yy, xs, zz].astype(F32),
                                     tc[(zz, *planar(n, xs, yy))].astype(F32)], axis=0)
                row = pl.ds(pl.multiple_of(zz * 288 + yy * ROWS, 8), ROWS)
                stage[row, 0:128] = v[:ROWS]
                stage[row, 128:256] = v[ROWS:]
                return carry
            lax.fori_loop(0, 16, unpack, 0)
            dcol[SLAB * xs:SLAB * (xs + 1), :] = stage[...].astype(BF16)

        def tokens(m):
            rows = pl.ds(m * LEN, LEN)
            spread[rows, :] = jnp.dot(xv[rows, :], dcol[...], preferred_element_type=F32)
        tokens(0)
        tokens(1)

    def make_signal(n):
        cols = slice(WIDE * n, WIDE * (n + 1))

        def tokens(m, carry):
            rows = pl.ds(pl.multiple_of(m * 256, 256), 256)
            u = cot[rows, cols].astype(F32) + kl_weight * spread[rows, :]
            lane = pl.ds(pl.multiple_of((m % 3) * 256, 256), 256)
            w = scale[m // 3, 0:1, lane]
            sig_t[cols, rows] = (u.T * w).astype(BF16)
            return carry
        lax.fori_loop(0, 6, tokens, 0)

    near = jnp.where(x % 2 == 0, 1, 3)
    order = (2, 4 - near, near, 0)
    heavy = [[None, [], None], [None, [], None]]

    def second_product(n, i):
        ga, gb, gc, ra, rb, rc = lanes[n][3:9]
        p, q, _ = CUTS[n]
        off = order[i]
        xs = (x + off) % 4
        out = jnp.dot(sig_t[WIDE * n:WIDE * (n + 1), :], xv[:, pl.ds(pl.multiple_of(xs * SLAB, 128), SLAB)],
                      preferred_element_type=F32)
        stage[...] = out.T

        def pack(m, carry):
            yy, zz = m // 4, m % 4
            row = pl.ds(pl.multiple_of(zz * 288 + yy * ROWS, 8), ROWS)
            v = jnp.concatenate([stage[row, 0:128], stage[row, 128:256]], axis=0)
            g32[n, xs, zz, yy] = v
            ga[xs, yy, zz] = v[:p].astype(BF16)
            gb[yy, xs, zz] = v[p:p + q].astype(BF16)
            gc[(zz, *planar(n, xs, yy))] = v[p + q:].astype(BF16)
            return carry
        lax.fori_loop(0, 16, pack, 0)
        if i == 0:
            heavy[n][0], heavy[n][2] = Group(ra), Group(rc)
        if i < 3:
            heavy[n][0].push(ga.at[xs], ra.at[off - 1], on_x(off))
        heavy[n][1].append(Group(rb.at[:, 0]))
        for k in (2, 1, 3):
            heavy[n][1][i].push(gb.at[(y + k) % 4, xs], rb.at[k - 1, xs], on_y(k))
        if i % 2:
            pair = pl.ds((xs // 2) * 2, 2)
            for k in (4, 3, 5, 2, 6, 1, 7):
                there = (z + k) % 8
                window = pl.ds(pl.multiple_of((there % 2) * 16, 16), 16)
                if n:
                    heavy[n][2].push(gc.at[there // 2, :, pair, window], rc.at[k - 1, :, pair], on_z(k))
                else:
                    heavy[n][2].push(gc.at[there // 2, pair, :, window], rc.at[k - 1, pair], on_z(k))

    middle = [None, None]

    def first_sums(n):
        ra, rb, rc, ha, hb, hc, r2a, r2b, r2c = lanes[n][6:15]
        ha, ha16 = ha
        hb, hb16 = hb
        hc, hc16 = hc
        p, q, _ = CUTS[n]
        middle[n] = [Group(r2a), Group(r2b), Group(r2c)]
        for i, off in enumerate(order):
            xs = (x + off) % 4
            heavy[n][1][i].arrive()

            def sum_b(zz, carry):
                t = g32[n, xs, zz, y, p:p + q, :]
                for k in range(3):
                    t = t + rb[k, xs, zz].astype(F32)
                hb[xs, zz] = t
                hb16[xs, zz] = t.astype(BF16)
                return carry
            lax.fori_loop(0, 4, sum_b, 0)
            if i < 3:
                middle[n][1].push(hb16.at[xs], r2b.at[off - 1], on_x(off))
        heavy[n][0].arrive()
        for off in (2, 1, 3, 0):
            yy = (y + off) % 4

            def sum_a(zz, carry):
                t = g32[n, x, zz, yy, :p, :]
                for k in range(3):
                    t = t + ra[k, yy, zz].astype(F32)
                ha[yy, zz] = t
                ha16[yy, zz] = t.astype(BF16)
                return carry
            lax.fori_loop(0, 4, sum_a, 0)
            if off:
                middle[n][0].push(ha16.at[yy], r2a.at[off - 1], on_y(off))
        heavy[n][2].arrive()
        for off in (2, 1, 3, 0):
            slow = (planar(n, x, y)[0] + off) % 4

            def sum_c(fast, carry):
                xs, yy = planar(n, slow, fast)
                t = g32[n, xs, zh, yy, pl.ds(pl.multiple_of(p + q + zl * 16, 8), 16), :]
                for k in range(7):
                    t = t + rc[k, slow, fast].astype(F32)
                hc[slow, fast] = t
                hc16[slow, fast] = t.astype(BF16)
                return carry
            lax.fori_loop(0, 4, sum_c, 0)
            if off:
                middle[n][2].push(hc16.at[slow], r2c.at[off - 1], on_slow[n](off))

    last = [None, None]

    def second_sums(n):
        (ha, _), (hb, _), (hc, _), r2a, r2b, r2c, (js, jc), (r3, r3c) = lanes[n][9:17]
        js, js16 = js
        jc, jc16 = jc
        p, q, _ = CUTS[n]
        last[n] = [Group(r3), Group(r3c)]
        for group in middle[n]:
            group.arrive()

        def sum_ab(zz, carry):
            a, b = ha[y, zz], hb[x, zz]
            for k in range(3):
                a = a + r2a[k, zz].astype(F32)
                b = b + r2b[k, zz].astype(F32)
            for side in range(2):
                s, t = (p - 32) * side, (q - 32) * side
                v = jnp.concatenate([a[s:s + 32], b[t:t + 32]], axis=0)
                js[zz, side] = v
                js16[zz, side] = v.astype(BF16)
            return carry
        lax.fori_loop(0, 4, sum_ab, 0)
        for k in (4, 3, 5, 2, 6, 1, 7):
            there = (z + k) % 8
            last[n][0].push(js16.at[there // 2, there % 2], r3.at[k - 1], on_z(k))
        slow, fast = planar(n, x, y)
        for there in range(4):
            t = hc[slow, there]
            for k in range(3):
                t = t + r2c[k, there].astype(F32)
            jc[there] = t
            jc16[there] = t.astype(BF16)
        for k in (2, 1, 3):
            last[n][1].push(jc16.at[(fast + k) % 4], r3c.at[k - 1], on_fast[n](k))

    done = [None, None]

    def last_sums(n):
        (js, jc), (r3, r3c) = lanes[n][15:17]
        last[n][0].arrive()
        t = js[0][zh, zl]
        for k in range(7):
            t = t + r3[k].astype(F32)
        last[n][1].arrive()
        u = jc[0][planar(n, x, y)[1]]
        for k in range(3):
            u = u + r3c[k].astype(F32)
        fin[n, c * 2 + zl] = jnp.concatenate([t, u], axis=0)
        done[n] = spread_out(fin.at[0, three], fin.at[n, c * 2 + zl], (diagonal, partner, sibling))

    def finish(n):
        done[n].arrive()
        p, q, _ = CUTS[n]
        for core in range(2):
            lo, hi = fin[n, core * 2], fin[n, core * 2 + 1]
            v = jnp.concatenate([lo[0:32], hi[64 - p + 32 - 32:32], lo[32:64], hi[64 - q + 32:64],
                                 lo[64:80], hi[64:80]], axis=0)
            for half in range(2):
                begin = core * HALF + n * WIDE + half * 128
                cols = slice(begin, begin + 128)
                g = v[ROWS * half:ROWS * (half + 1)]
                grad_ref[:, cols] = g
                next_ref[:, cols] = (1.0 - ema_rate) * anchor_ref[:, cols] + ema_rate * (
                    policy_ref[:, cols] - step_size * g)

    started = third_start(0)
    rest0 = third_forward(0, started)
    started = third_start(1)
    own_x.wait()
    own_cot.wait()
    for group in sib:
        group.arrive()
    for group in rest0:
        group.arrive()
    first_product(0)
    rest1 = third_forward(1, started)
    make_signal(0)
    for i in range(4):
        second_product(0, i)
    for group in rest1:
        group.arrive()
    first_product(1)
    make_signal(1)
    for i in range(3):
        second_product(1, i)
    first_sums(0)
    second_product(1, 3)
    second_sums(0)
    first_sums(1)
    last_sums(0)
    second_sums(1)
    finish(0)
    last_sums(1)
    finish(1)

    for group in groups:
        group.sent()


def shards(inputs, cotangent, response_mask, policy, anchor):
    vmem = pl.BlockSpec(memory_space=pltpu.VMEM)
    hbm = pl.BlockSpec(memory_space=pl.ANY)
    scratch = [
        pltpu.VMEM((2 * LEN, D), BF16),
        pltpu.VMEM((SLAB, WIDE), F32),
        pltpu.VMEM((D, WIDE), BF16),
        pltpu.VMEM((2 * LEN, WIDE), F32),
        pltpu.VMEM((2 * LEN, HALF), BF16),
        pltpu.VMEM((HALF, 2 * LEN), BF16),
        pltpu.VMEM((2, 8, LEN), F32),
        pltpu.VMEM((2, 4, 4, 4, PACK, 128), F32),
        pltpu.VMEM((2, 4, 80, 128), F32),
    ]
    for p, q, r in CUTS:
        scratch += [pltpu.VMEM((4, 4, 4, m, 128), BF16) for m in (p, q, r)]
        scratch += [pltpu.VMEM((4, 4, 4, m, 128), BF16) for m in (p, q, r)]
        scratch += [pltpu.VMEM((3, 4, 4, m, 128), BF16) for m in (p, q)]
        scratch += [pltpu.VMEM((7, 4, 4, 16, 128), BF16)]
        scratch += [(pltpu.VMEM((4, 4, m, 128), F32), pltpu.VMEM((4, 4, m, 128), BF16))
                    for m in (p, q, 16)]
        scratch += [pltpu.VMEM((3, 4, m, 128), BF16) for m in (p, q, 16)]
        scratch += [((pltpu.VMEM((4, 2, 64, 128), F32), pltpu.VMEM((4, 2, 64, 128), BF16)),
                     (pltpu.VMEM((4, 16, 128), F32), pltpu.VMEM((4, 16, 128), BF16)))]
        scratch += [(pltpu.VMEM((7, 64, 128), BF16), pltpu.VMEM((3, 16, 128), BF16))]
    scratch += [pltpu.SemaphoreType.DMA((NSEM,)), pltpu.SemaphoreType.DMA((NSEM,)),
                pltpu.SemaphoreType.DMA((2,))]
    rows = jax.ShapeDtypeStruct((ROWS, KVW), F32)
    return pl.pallas_call(
        kernel,
        out_shape=(rows, rows),
        in_specs=[hbm, hbm, vmem, vmem, vmem],
        out_specs=(vmem, vmem),
        scratch_shapes=scratch,
        compiler_params=pltpu.CompilerParams(
            collective_id=0, has_side_effects=True, vmem_limit_bytes=62 * 2**20),
        cost_estimate=pl.CostEstimate(flops=4 * LEN * D * KVW, bytes_accessed=20 * 2**20, transcendentals=0),
        name="policy_step",
    )(inputs, cotangent, response_mask, policy, anchor)


def solution(mesh):
    placed = (
        P(("dp", "fsdp"), None, None),
        P(("dp", "fsdp"), None, None),
        P(("dp", "fsdp"), None),
        P("fsdp", None),
        P("fsdp", None),
    )
    return jax.shard_map(
        shards,
        mesh=mesh,
        in_specs=placed,
        out_specs=(P("fsdp", None), P("fsdp", None)),
        check_vma=False,
    )
```

```python
import jax
import jax.numpy as jnp
from jax import lax
from jax.experimental import pallas as pl
from jax.experimental.pallas import tpu as pltpu
from jax.sharding import PartitionSpec as P

kl_weight = 0.5
ema_rate = 0.01
step_size = 0.1

MESH = pl.DeviceIdType.MESH
F32 = jnp.float32
BF16 = jnp.bfloat16

LEN = 768
D = 4608
KVW = 1024
HALF = KVW // 2
WIDE = HALF // 2
ROWS = 72
SLAB = 16 * ROWS
PACK = 2 * ROWS
CUTS = ((64, 48, 32), (48, 64, 32))
AG = ((64, 64, 16), (64, 64, 16))
NSEM = 64


def kernel(x_hbm, cot_hbm, mask_hbm, policy_hbm, anchor_hbm, grad_ref, next_ref,
           mask_ref, policy_ref, anchor_ref, xv, stage, dcol, spread, cot, sig_t, scale, g32, fin, *rest):
    lanes = [rest[17 * i:17 * (i + 1)] for i in range(2)]
    ssem, rsem, loc = rest[34:]
    dp, fs = lax.axis_index("dp"), lax.axis_index("fsdp")
    c, zl = dp % 2, dp // 2
    x, zh, y = fs // 16, (fs // 4) % 4, fs % 4
    z = zh * 2 + zl

    def at(c_, x_, y_, z_):
        return ((z_ % 2) * 2 + c_, (x_ * 4 + z_ // 2) * 4 + y_)

    def on_x(k):
        return at(c, (x + k) % 4, y, z)

    def on_y(k):
        return at(c, x, (y + k) % 4, z)

    def on_z(k):
        return at(c, x, y, (z + k) % 8)

    def on_pairs(k):
        return on_z(jnp.where(zl == 1, k, 8 - k))

    sibling = at(1 - c, x, y, z)
    partner = at(c, x, y, zh * 2 + (1 - zl))
    diagonal = at(1 - c, x, y, zh * 2 + (1 - zl))

    groups = []

    class Group:
        def __init__(self, span):
            self.span, self.n = span, len(groups)
            groups.append(self)

        def push(self, src, dst, device):
            pltpu.make_async_remote_copy(
                src_ref=src, dst_ref=dst, send_sem=ssem.at[self.n], recv_sem=rsem.at[self.n],
                device_id=device, device_id_type=MESH).start()

        def arrive(self):
            pltpu.make_async_copy(self.span, self.span, rsem.at[self.n]).wait()

        def sent(self):
            pltpu.make_async_copy(self.span, self.span, ssem.at[self.n]).wait()

    def spread_out(span, ref, targets):
        group = Group(span)
        for device in targets:
            group.push(ref, ref, device)
        return group

    def planar(n, xs, yy):
        return (xs, yy) if n else (yy, xs)

    on_slow, on_fast = (on_y, on_x), (on_x, on_y)

    small = [pltpu.make_async_copy(src, dst, loc.at[2 + n]) for n, (src, dst) in enumerate((
        (policy_hbm, policy_ref), (anchor_hbm, anchor_ref), (mask_hbm, mask_ref)))]
    for copy in small:
        copy.start()
    own_x = pltpu.make_async_copy(x_hbm.at[0], xv.at[pl.ds(0, LEN)], loc.at[0])
    own_x.start()
    mine = pl.multiple_of(c * HALF, HALF)
    other = pl.multiple_of((1 - c) * HALF, HALF)
    own_cot = pltpu.make_async_copy(
        cot_hbm.at[0, :, pl.ds(mine, HALF)], cot.at[pl.ds(0, LEN)], loc.at[1])
    own_cot.start()

    barrier = pltpu.get_barrier_semaphore()
    peers = [on_x(k) for k in (1, 2, 3)] + [on_y(k) for k in (1, 2, 3)]
    peers += [on_z(k) for k in range(1, 8)] + [sibling, diagonal]
    for device in peers:
        pl.semaphore_signal(barrier, inc=1, device_id=device, device_id_type=MESH)

    for copy in small:
        copy.wait()
    delta = policy_ref[...] - anchor_ref[...]
    delta = jnp.where(c == 0, delta[:, :HALF], delta[:, HALF:])
    for n, (ta, tb, tc, *_) in enumerate(lanes):
        p, q, _ = AG[n]
        v = jnp.concatenate([delta[:, WIDE * n:WIDE * n + 128], delta[:, WIDE * n + 128:WIDE * n + 256]], axis=0)
        ta[x, y, zh] = v[:p].astype(BF16)
        tb[y, x, zh] = v[p:p + q].astype(BF16)
        tc[(zh, *planar(n, x, y))] = v[p + q:].astype(BF16)
    weights = mask_ref[...].astype(F32)
    weights = weights / jnp.sum(weights, axis=1, keepdims=True)
    scale[0] = jnp.broadcast_to(weights, (8, LEN))

    pl.semaphore_wait(barrier, len(peers))

    three = pl.ds(0, 3)
    first = []
    for n, (ta, tb, tc, *_) in enumerate(lanes):
        first.append([
            spread_out(ta.at[0, 0, three], ta.at[x, y, zh], [on_pairs(k) for k in (1, 2, 3)]),
            spread_out(tb.at[0, 0, three], tb.at[y, x, zh], [on_pairs(k) for k in (1, 2, 3)]),
            spread_out(tc.at[0, 0, three], tc.at[(zh, *planar(n, x, y))],
                       [on_fast[n](k) for k in (1, 2, 3)])])

    sib = [Group(xv.at[pl.ds(LEN, LEN)]), Group(cot.at[pl.ds(LEN, LEN)]), Group(scale.at[1])]
    sib[0].push(x_hbm.at[0], xv.at[pl.ds(LEN, LEN)], sibling)
    sib[1].push(cot_hbm.at[0, :, pl.ds(other, HALF)], cot.at[pl.ds(LEN, LEN)], sibling)
    sib[2].push(scale.at[0], scale.at[1], sibling)

    def second_start(n):
        ta, tb, tc = lanes[n][:3]
        first[n][0].arrive()
        pa = spread_out(ta.at[0, three], ta.at[x, y], [on_y(k) for k in (1, 2, 3)])
        first[n][1].arrive()
        pb = spread_out(tb.at[0, three], tb.at[y, x], [on_x(k) for k in (1, 2, 3)])
        first[n][2].arrive()
        pc = spread_out(tc.at[0, three], tc.at[zh, planar(n, x, y)[0]], [on_slow[n](k) for k in (1, 2, 3)])
        return pa, pb, pc

    front, back = pl.ds(0, 2), pl.ds(2, 2)

    def ring_start(t, me, on):
        one, two = Group(t.at[0]), Group(t.at[0])
        for group, rows, k in ((one, front, 1), (one, back, 3), (two, back, 1), (two, front, 3)):
            group.push(t.at[me, rows], t.at[me, rows], on(k))
        return one, two

    def ring_forward(t, me, on, started):
        started[0].arrive()
        group = Group(t.at[0])
        for owner, rows, k in (((me + 3) % 4, front, 1), ((me + 1) % 4, back, 3)):
            group.push(t.at[owner, rows], t.at[owner, rows], on(k))
        return started[1], group

    def third_start(n, second):
        ta, tb, tc = lanes[n][:3]
        second[0].arrive()
        a = ring_start(ta, x, on_x)
        second[1].arrive()
        b = ring_start(tb, y, on_y)
        second[2].arrive()
        c1 = [spread_out(tc.at[0, half], tc.at[zh, half], [on_pairs(1)]) for half in (front, back)]
        return a, b, c1

    def third_forward(n, started):
        ta, tb, tc = lanes[n][:3]
        a, b, c1 = started
        a = ring_forward(ta, x, on_x, a)
        b = ring_forward(tb, y, on_y, b)
        relay = Group(tc.at[pl.ds(0, 2)])
        owner = (zh + jnp.where(zl == 1, 1, 3)) % 4
        for group, half in zip(c1, (front, back)):
            group.arrive()
            for k in (1, 2):
                relay.push(tc.at[owner, half], tc.at[owner, half], on_z(jnp.where(zl == 1, 8 - k, k)))
        return (*a, *b, relay)

    def first_product(n):
        ta, tb, tc = lanes[n][:3]
        for xs in range(4):
            def unpack(i, carry):
                yy, zz = i // 4, i % 4
                v = jnp.concatenate([ta[xs, yy, zz].astype(F32), tb[yy, xs, zz].astype(F32),
                                     tc[(zz, *planar(n, xs, yy))].astype(F32)], axis=0)
                row = pl.ds(pl.multiple_of(zz * 288 + yy * ROWS, 8), ROWS)
                stage[row, 0:128] = v[:ROWS]
                stage[row, 128:256] = v[ROWS:]
                return carry
            lax.fori_loop(0, 16, unpack, 0)
            dcol[SLAB * xs:SLAB * (xs + 1), :] = stage[...].astype(BF16)

        def tokens(m):
            rows = pl.ds(m * LEN, LEN)
            spread[rows, :] = jnp.dot(xv[rows, :], dcol[...], preferred_element_type=F32)
        tokens(0)
        tokens(1)

    def make_signal(n):
        cols = slice(WIDE * n, WIDE * (n + 1))

        def tokens(m, carry):
            rows = pl.ds(pl.multiple_of(m * 256, 256), 256)
            u = cot[rows, cols].astype(F32) + kl_weight * spread[rows, :]
            lane = pl.ds(pl.multiple_of((m % 3) * 256, 256), 256)
            w = scale[m // 3, 0:1, lane]
            sig_t[cols, rows] = (u.T * w).astype(BF16)
            return carry
        lax.fori_loop(0, 6, tokens, 0)

    near = jnp.where(x % 2 == 0, 1, 3)
    order = (2, 4 - near, near, 0)
    heavy = [[None, [], None], [None, [], None]]

    def second_product(n, i):
        ga, gb, gc, ra, rb, rc = lanes[n][3:9]
        p, q, _ = CUTS[n]
        off = order[i]
        xs = (x + off) % 4
        out = jnp.dot(sig_t[WIDE * n:WIDE * (n + 1), :], xv[:, pl.ds(pl.multiple_of(xs * SLAB, 128), SLAB)],
                      preferred_element_type=F32)
        stage[...] = out.T

        def pack(m, carry):
            yy, zz = m // 4, m % 4
            row = pl.ds(pl.multiple_of(zz * 288 + yy * ROWS, 8), ROWS)
            v = jnp.concatenate([stage[row, 0:128], stage[row, 128:256]], axis=0)
            g32[n, xs, zz, yy] = v
            ga[xs, yy, zz] = v[:p].astype(BF16)
            gb[yy, xs, zz] = v[p:p + q].astype(BF16)
            gc[(zz, *planar(n, xs, yy))] = v[p + q:].astype(BF16)
            return carry
        lax.fori_loop(0, 16, pack, 0)
        if i == 0:
            heavy[n][0], heavy[n][2] = Group(ra), [] if n else [Group(rc)]
        if i < 3:
            heavy[n][0].push(ga.at[xs], ra.at[off - 1], on_x(off))
        heavy[n][1].append(Group(rb.at[:, 0]))
        for k in (2, 1, 3):
            heavy[n][1][i].push(gb.at[(y + k) % 4, xs], rb.at[k - 1, xs], on_y(k))
        if n:
            heavy[n][2].append(Group(rc.at[:, 0]))
        for k in (4, 3, 5, 2, 6, 1, 7):
            there = (z + k) % 8
            window = pl.ds(pl.multiple_of((there % 2) * 16, 16), 16)
            if n:
                heavy[n][2][i].push(gc.at[there // 2, xs, :, window], rc.at[k - 1, xs], on_z(k))
            else:
                heavy[n][2][0].push(gc.at[there // 2, :, xs, window], rc.at[k - 1, :, xs], on_z(k))

    middle = [None, None]

    def first_sums(n):
        ra, rb, rc, ha, hb, hc, r2a, r2b, r2c = lanes[n][6:15]
        ha, ha16 = ha
        hb, hb16 = hb
        hc, hc16 = hc
        p, q, _ = CUTS[n]
        middle[n] = [Group(r2a), Group(r2b), Group(r2c)]

        def part_b(i):
            xs = (x + order[i]) % 4
            heavy[n][1][i].arrive()

            def sum_b(zz, carry):
                t = g32[n, xs, zz, y, p:p + q, :]
                for k in range(3):
                    t = t + rb[k, xs, zz].astype(F32)
                hb[xs, zz] = t
                hb16[xs, zz] = t.astype(BF16)
                return carry
            lax.fori_loop(0, 4, sum_b, 0)
            if i < 3:
                middle[n][1].push(hb16.at[xs], r2b.at[order[i] - 1], on_x(order[i]))

        def part_a():
            heavy[n][0].arrive()
            for off in (2, 1, 3, 0):
                yy = (y + off) % 4

                def sum_a(zz, carry):
                    t = g32[n, x, zz, yy, :p, :]
                    for k in range(3):
                        t = t + ra[k, yy, zz].astype(F32)
                    ha[yy, zz] = t
                    ha16[yy, zz] = t.astype(BF16)
                    return carry
                lax.fori_loop(0, 4, sum_a, 0)
                if off:
                    middle[n][0].push(ha16.at[yy], r2a.at[off - 1], on_y(off))

        def part_c(i):
            if i < len(heavy[n][2]):
                heavy[n][2][i].arrive()
            slow = (planar(n, x, y)[0] + order[i]) % 4

            def sum_c(fast, carry):
                xs, yy = planar(n, slow, fast)
                t = g32[n, xs, zh, yy, pl.ds(pl.multiple_of(p + q + zl * 16, 8), 16), :]
                for k in range(7):
                    t = t + rc[k, slow, fast].astype(F32)
                hc[slow, fast] = t
                hc16[slow, fast] = t.astype(BF16)
                return carry
            lax.fori_loop(0, 4, sum_c, 0)
            if i < 3:
                middle[n][2].push(hc16.at[slow], r2c.at[order[i] - 1], on_slow[n](order[i]))

        for i in range(3):
            part_b(i)
        part_a()
        for i in range(3):
            part_c(i)
        part_b(3)
        part_c(3)

    last = [None, None]

    def second_sums(n):
        (ha, _), (hb, _), (hc, _), r2a, r2b, r2c, (js, jc), (r3, r3c) = lanes[n][9:17]
        js, js16 = js
        jc, jc16 = jc
        p, q, _ = CUTS[n]
        last[n] = [Group(r3), Group(r3c)]
        for group in middle[n]:
            group.arrive()

        def sum_ab(zz, carry):
            a, b = ha[y, zz], hb[x, zz]
            for k in range(3):
                a = a + r2a[k, zz].astype(F32)
                b = b + r2b[k, zz].astype(F32)
            for side in range(2):
                s, t = (p - 32) * side, (q - 32) * side
                v = jnp.concatenate([a[s:s + 32], b[t:t + 32]], axis=0)
                js[zz, side] = v
                js16[zz, side] = v.astype(BF16)
            return carry
        lax.fori_loop(0, 4, sum_ab, 0)
        for k in (4, 3, 5, 2, 6, 1, 7):
            there = (z + k) % 8
            last[n][0].push(js16.at[there // 2, there % 2], r3.at[k - 1], on_z(k))
        slow, fast = planar(n, x, y)
        for there in range(4):
            t = hc[slow, there]
            for k in range(3):
                t = t + r2c[k, there].astype(F32)
            jc[there] = t
            jc16[there] = t.astype(BF16)
        for k in (2, 1, 3):
            last[n][1].push(jc16.at[(fast + k) % 4], r3c.at[k - 1], on_fast[n](k))

    done = [None, None]

    def last_sums(n):
        (js, jc), (r3, r3c) = lanes[n][15:17]
        last[n][0].arrive()
        t = js[0][zh, zl]
        for k in range(7):
            t = t + r3[k].astype(F32)
        last[n][1].arrive()
        u = jc[0][planar(n, x, y)[1]]
        for k in range(3):
            u = u + r3c[k].astype(F32)
        fin[n, c * 2 + zl] = jnp.concatenate([t, u], axis=0)
        done[n] = spread_out(fin.at[0, three], fin.at[n, c * 2 + zl], (diagonal, partner, sibling))

    def finish(n):
        done[n].arrive()
        p, q, _ = CUTS[n]
        for core in range(2):
            lo, hi = fin[n, core * 2], fin[n, core * 2 + 1]
            v = jnp.concatenate([lo[0:32], hi[64 - p + 32 - 32:32], lo[32:64], hi[64 - q + 32:64],
                                 lo[64:80], hi[64:80]], axis=0)
            for half in range(2):
                begin = core * HALF + n * WIDE + half * 128
                cols = slice(begin, begin + 128)
                g = v[ROWS * half:ROWS * (half + 1)]
                grad_ref[:, cols] = g
                next_ref[:, cols] = (1.0 - ema_rate) * anchor_ref[:, cols] + ema_rate * (
                    policy_ref[:, cols] - step_size * g)

    second = second_start(0)
    started = third_start(0, second)
    second = second_start(1)
    rest0 = third_forward(0, started)
    started = third_start(1, second)
    own_x.wait()
    own_cot.wait()
    for group in sib:
        group.arrive()
    for group in rest0:
        group.arrive()
    first_product(0)
    make_signal(0)
    rest1 = third_forward(1, started)
    for i in range(4):
        second_product(0, i)
    for group in rest1:
        group.arrive()
    first_product(1)
    make_signal(1)
    for i in range(3):
        second_product(1, i)
    first_sums(0)
    second_product(1, 3)
    first_sums(1)
    second_sums(0)
    second_sums(1)
    last_sums(0)
    last_sums(1)
    finish(0)
    finish(1)

    for group in groups:
        group.sent()


def shards(inputs, cotangent, response_mask, policy, anchor):
    vmem = pl.BlockSpec(memory_space=pltpu.VMEM)
    hbm = pl.BlockSpec(memory_space=pl.ANY)
    scratch = [
        pltpu.VMEM((1, LEN), jnp.int32),
        pltpu.VMEM((ROWS, KVW), F32),
        pltpu.VMEM((ROWS, KVW), F32),
        pltpu.VMEM((2 * LEN, D), BF16),
        pltpu.VMEM((SLAB, WIDE), F32),
        pltpu.VMEM((D, WIDE), BF16),
        pltpu.VMEM((2 * LEN, WIDE), F32),
        pltpu.VMEM((2 * LEN, HALF), BF16),
        pltpu.VMEM((HALF, 2 * LEN), BF16),
        pltpu.VMEM((2, 8, LEN), F32),
        pltpu.VMEM((2, 4, 4, 4, PACK, 128), F32),
        pltpu.VMEM((2, 4, 80, 128), F32),
    ]
    for ag, (p, q, r) in zip(AG, CUTS):
        scratch += [pltpu.VMEM((4, 4, 4, m, 128), BF16) for m in ag]
        scratch += [pltpu.VMEM((4, 4, 4, m, 128), BF16) for m in (p, q, r)]
        scratch += [pltpu.VMEM((3, 4, 4, m, 128), BF16) for m in (p, q)]
        scratch += [pltpu.VMEM((7, 4, 4, 16, 128), BF16)]
        scratch += [(pltpu.VMEM((4, 4, m, 128), F32), pltpu.VMEM((4, 4, m, 128), BF16))
                    for m in (p, q, 16)]
        scratch += [pltpu.VMEM((3, 4, m, 128), BF16) for m in (p, q, 16)]
        scratch += [((pltpu.VMEM((4, 2, 64, 128), F32), pltpu.VMEM((4, 2, 64, 128), BF16)),
                     (pltpu.VMEM((4, 16, 128), F32), pltpu.VMEM((4, 16, 128), BF16)))]
        scratch += [(pltpu.VMEM((7, 64, 128), BF16), pltpu.VMEM((3, 16, 128), BF16))]
    scratch += [pltpu.SemaphoreType.DMA((NSEM,)), pltpu.SemaphoreType.DMA((NSEM,)),
                pltpu.SemaphoreType.DMA((5,))]
    rows = jax.ShapeDtypeStruct((ROWS, KVW), F32)
    return pl.pallas_call(
        kernel,
        out_shape=(rows, rows),
        in_specs=[hbm] * 5,
        out_specs=(vmem, vmem),
        scratch_shapes=scratch,
        compiler_params=pltpu.CompilerParams(
            collective_id=0, has_side_effects=True, vmem_limit_bytes=62 * 2**20),
        cost_estimate=pl.CostEstimate(flops=4 * LEN * D * KVW, bytes_accessed=20 * 2**20, transcendentals=0),
        name="policy_step",
    )(inputs, cotangent, response_mask, policy, anchor)


def solution(mesh):
    placed = (
        P(("dp", "fsdp"), None, None),
        P(("dp", "fsdp"), None, None),
        P(("dp", "fsdp"), None),
        P("fsdp", None),
        P("fsdp", None),
    )
    return jax.shard_map(
        shards,
        mesh=mesh,
        in_specs=placed,
        out_specs=(P("fsdp", None), P("fsdp", None)),
        check_vma=False,
    )
```

```python
import jax
import jax.numpy as jnp
from jax import lax
from jax.experimental import pallas as pl
from jax.experimental.pallas import tpu as pltpu
from jax.sharding import PartitionSpec as P

kl_weight = 0.5
ema_rate = 0.01
step_size = 0.1

MESH = pl.DeviceIdType.MESH
F32 = jnp.float32
BF16 = jnp.bfloat16

LEN = 768
D = 4608
KVW = 1024
HALF = KVW // 2
WIDE = HALF // 2
ROWS = 72
SLAB = 16 * ROWS
PACK = 2 * ROWS
CUTS = ((64, 48, 32), (48, 64, 32))
AG = ((64, 64, 16), (64, 64, 16))
NSEM = 64


def kernel(x_hbm, cot_hbm, mask_hbm, policy_hbm, anchor_hbm, grad_ref, next_ref,
           mask_ref, policy_ref, anchor_ref, xv, stage, dcol, spread, cot, sig_t, scale, g32, fin, *rest):
    lanes = [rest[17 * i:17 * (i + 1)] for i in range(2)]
    ssem, rsem, loc = rest[34:]
    dp, fs = lax.axis_index("dp"), lax.axis_index("fsdp")
    c, zl = dp % 2, dp // 2
    x, zh, y = fs // 16, (fs // 4) % 4, fs % 4
    z = zh * 2 + zl

    def at(c_, x_, y_, z_):
        return ((z_ % 2) * 2 + c_, (x_ * 4 + z_ // 2) * 4 + y_)

    def on_x(k):
        return at(c, (x + k) % 4, y, z)

    def on_y(k):
        return at(c, x, (y + k) % 4, z)

    def on_z(k):
        return at(c, x, y, (z + k) % 8)

    def on_pairs(k):
        return on_z(jnp.where(zl == 1, k, 8 - k))

    sibling = at(1 - c, x, y, z)
    partner = at(c, x, y, zh * 2 + (1 - zl))
    diagonal = at(1 - c, x, y, zh * 2 + (1 - zl))

    groups = []

    class Group:
        def __init__(self, span):
            self.span, self.n = span, len(groups)
            groups.append(self)

        def push(self, src, dst, device):
            pltpu.make_async_remote_copy(
                src_ref=src, dst_ref=dst, send_sem=ssem.at[self.n], recv_sem=rsem.at[self.n],
                device_id=device, device_id_type=MESH).start()

        def arrive(self):
            pltpu.make_async_copy(self.span, self.span, rsem.at[self.n]).wait()

        def sent(self):
            pltpu.make_async_copy(self.span, self.span, ssem.at[self.n]).wait()

    def spread_out(span, ref, targets):
        group = Group(span)
        for device in targets:
            group.push(ref, ref, device)
        return group

    def planar(n, xs, yy):
        return (xs, yy) if n else (yy, xs)

    on_slow, on_fast = (on_y, on_x), (on_x, on_y)

    small = [pltpu.make_async_copy(src, dst, loc.at[2 + n]) for n, (src, dst) in enumerate((
        (policy_hbm, policy_ref), (anchor_hbm, anchor_ref), (mask_hbm, mask_ref)))]
    for copy in small:
        copy.start()
    own_x = pltpu.make_async_copy(x_hbm.at[0], xv.at[pl.ds(0, LEN)], loc.at[0])
    own_x.start()
    mine = pl.multiple_of(c * HALF, HALF)
    other = pl.multiple_of((1 - c) * HALF, HALF)
    own_cot = pltpu.make_async_copy(
        cot_hbm.at[0, :, pl.ds(mine, HALF)], cot.at[pl.ds(0, LEN)], loc.at[1])
    own_cot.start()

    barrier = pltpu.get_barrier_semaphore()
    peers = [on_x(k) for k in (1, 2, 3)] + [on_y(k) for k in (1, 2, 3)]
    peers += [on_z(k) for k in range(1, 8)] + [sibling, diagonal]
    for device in peers:
        pl.semaphore_signal(barrier, inc=1, device_id=device, device_id_type=MESH)

    for copy in small:
        copy.wait()
    delta = policy_ref[...] - anchor_ref[...]
    delta = jnp.where(c == 0, delta[:, :HALF], delta[:, HALF:])
    for n, (ta, tb, tc, *_) in enumerate(lanes):
        p, q, _ = AG[n]
        v = jnp.concatenate([delta[:, WIDE * n:WIDE * n + 128], delta[:, WIDE * n + 128:WIDE * n + 256]], axis=0)
        ta[x, y, zh] = v[:p].astype(BF16)
        tb[y, x, zh] = v[p:p + q].astype(BF16)
        tc[(zh, *planar(n, x, y))] = v[p + q:].astype(BF16)
    weights = mask_ref[...].astype(F32)
    weights = weights / jnp.sum(weights, axis=1, keepdims=True)
    scale[0] = jnp.broadcast_to(weights, (8, LEN))

    pl.semaphore_wait(barrier, len(peers))

    three = pl.ds(0, 3)
    first = []
    for n, (ta, tb, tc, *_) in enumerate(lanes):
        first.append([
            spread_out(ta.at[0, 0, three], ta.at[x, y, zh], [on_pairs(k) for k in (1, 2, 3)]),
            spread_out(tb.at[0, 0, three], tb.at[y, x, zh], [on_pairs(k) for k in (1, 2, 3)]),
            spread_out(tc.at[0, 0, three], tc.at[(zh, *planar(n, x, y))],
                       [on_fast[n](k) for k in (1, 2, 3)])])

    sib = [Group(xv.at[pl.ds(LEN, LEN)]), Group(cot.at[pl.ds(LEN, LEN)]), Group(scale.at[1])]
    sib[0].push(x_hbm.at[0], xv.at[pl.ds(LEN, LEN)], sibling)
    sib[1].push(cot_hbm.at[0, :, pl.ds(other, HALF)], cot.at[pl.ds(LEN, LEN)], sibling)
    sib[2].push(scale.at[0], scale.at[1], sibling)

    def second_start(n):
        ta, tb, tc = lanes[n][:3]
        first[n][0].arrive()
        pa = spread_out(ta.at[0, three], ta.at[x, y], [on_y(k) for k in (1, 2, 3)])
        first[n][1].arrive()
        pb = spread_out(tb.at[0, three], tb.at[y, x], [on_x(k) for k in (1, 2, 3)])
        first[n][2].arrive()
        pc = spread_out(tc.at[0, three], tc.at[zh, planar(n, x, y)[0]], [on_slow[n](k) for k in (1, 2, 3)])
        return pa, pb, pc

    front, back = pl.ds(0, 2), pl.ds(2, 2)

    def ring_start(t, me, on):
        one, two = Group(t.at[0]), Group(t.at[0])
        for group, rows, k in ((one, front, 1), (one, back, 3), (two, back, 1), (two, front, 3)):
            group.push(t.at[me, rows], t.at[me, rows], on(k))
        return one, two

    def ring_forward(t, me, on, started):
        started[0].arrive()
        group = Group(t.at[0])
        for owner, rows, k in (((me + 3) % 4, front, 1), ((me + 1) % 4, back, 3)):
            group.push(t.at[owner, rows], t.at[owner, rows], on(k))
        return started[1], group

    def third_start(n, second):
        ta, tb, tc = lanes[n][:3]
        second[0].arrive()
        a = ring_start(ta, x, on_x)
        second[1].arrive()
        b = ring_start(tb, y, on_y)
        second[2].arrive()
        c1 = [spread_out(tc.at[0, half], tc.at[zh, half], [on_pairs(1)]) for half in (front, back)]
        return a, b, c1

    def third_forward(n, started):
        ta, tb, tc = lanes[n][:3]
        a, b, c1 = started
        a = ring_forward(ta, x, on_x, a)
        b = ring_forward(tb, y, on_y, b)
        relay = Group(tc.at[pl.ds(0, 2)])
        owner = (zh + jnp.where(zl == 1, 1, 3)) % 4
        for group, half in zip(c1, (front, back)):
            group.arrive()
            for k in (1, 2):
                relay.push(tc.at[owner, half], tc.at[owner, half], on_z(jnp.where(zl == 1, 8 - k, k)))
        return (*a, *b, relay)

    def first_product(n):
        ta, tb, tc = lanes[n][:3]
        for xs in range(4):
            def unpack(i, carry):
                yy, zz = i // 4, i % 4
                v = jnp.concatenate([ta[xs, yy, zz].astype(F32), tb[yy, xs, zz].astype(F32),
                                     tc[(zz, *planar(n, xs, yy))].astype(F32)], axis=0)
                row = pl.ds(pl.multiple_of(zz * 288 + yy * ROWS, 8), ROWS)
                stage[row, 0:128] = v[:ROWS]
                stage[row, 128:256] = v[ROWS:]
                return carry
            lax.fori_loop(0, 16, unpack, 0)
            dcol[SLAB * xs:SLAB * (xs + 1), :] = stage[...].astype(BF16)

        def tokens(m):
            rows = pl.ds(m * LEN, LEN)
            spread[rows, :] = jnp.dot(xv[rows, :], dcol[...], preferred_element_type=F32)
        tokens(0)
        tokens(1)

    def make_signal(n):
        cols = slice(WIDE * n, WIDE * (n + 1))

        def tokens(m, carry):
            rows = pl.ds(pl.multiple_of(m * 256, 256), 256)
            u = cot[rows, cols].astype(F32) + kl_weight * spread[rows, :]
            lane = pl.ds(pl.multiple_of((m % 3) * 256, 256), 256)
            w = scale[m // 3, 0:1, lane]
            sig_t[cols, rows] = (u.T * w).astype(BF16)
            return carry
        lax.fori_loop(0, 6, tokens, 0)

    near = jnp.where(x % 2 == 0, 1, 3)
    order = (2, 4 - near, near, 0)
    heavy = [[None, [], None], [None, [], None]]

    def second_product(n, i):
        ga, gb, gc, ra, rb, rc = lanes[n][3:9]
        p, q, _ = CUTS[n]
        off = order[i]
        xs = (x + off) % 4
        out = jnp.dot(sig_t[WIDE * n:WIDE * (n + 1), :], xv[:, pl.ds(pl.multiple_of(xs * SLAB, 128), SLAB)],
                      preferred_element_type=F32)
        stage[...] = out.T

        def pack(m, carry):
            yy, zz = m // 4, m % 4
            row = pl.ds(pl.multiple_of(zz * 288 + yy * ROWS, 8), ROWS)
            v = jnp.concatenate([stage[row, 0:128], stage[row, 128:256]], axis=0)
            g32[n, xs, zz, yy] = v
            ga[xs, yy, zz] = v[:p].astype(BF16)
            gb[yy, xs, zz] = v[p:p + q].astype(BF16)
            gc[(zz, *planar(n, xs, yy))] = v[p + q:].astype(BF16)
            return carry
        lax.fori_loop(0, 16, pack, 0)
        if i == 0:
            heavy[n][0], heavy[n][2] = Group(ra), [] if n else [Group(rc)]
        if i < 3:
            heavy[n][0].push(ga.at[xs], ra.at[off - 1], on_x(off))
        heavy[n][1].append(Group(rb.at[:, 0]))
        for k in (2, 1, 3):
            heavy[n][1][i].push(gb.at[(y + k) % 4, xs], rb.at[k - 1, xs], on_y(k))
        if n:
            heavy[n][2].append(Group(rc.at[:, 0]))
        for k in (4, 3, 5, 2, 6, 1, 7):
            there = (z + k) % 8
            window = pl.ds(pl.multiple_of((there % 2) * 16, 16), 16)
            if n:
                heavy[n][2][i].push(gc.at[there // 2, xs, :, window], rc.at[k - 1, xs], on_z(k))
            else:
                heavy[n][2][0].push(gc.at[there // 2, :, xs, window], rc.at[k - 1, :, xs], on_z(k))

    middle = [None, None]

    def first_sums(n):
        ra, rb, rc, ha, hb, hc, r2a, r2b, r2c = lanes[n][6:15]
        ha, ha16 = ha
        hb, hb16 = hb
        hc, hc16 = hc
        p, q, _ = CUTS[n]
        middle[n] = [Group(r2a), Group(r2b), Group(r2c)]

        def part_b(i):
            xs = (x + order[i]) % 4
            heavy[n][1][i].arrive()

            def sum_b(zz, carry):
                t = g32[n, xs, zz, y, p:p + q, :]
                for k in range(3):
                    t = t + rb[k, xs, zz].astype(F32)
                hb[xs, zz] = t
                hb16[xs, zz] = t.astype(BF16)
                return carry
            lax.fori_loop(0, 4, sum_b, 0)
            if i < 3:
                middle[n][1].push(hb16.at[xs], r2b.at[order[i] - 1], on_x(order[i]))

        def part_a():
            heavy[n][0].arrive()
            for off in (2, 1, 3, 0):
                yy = (y + off) % 4

                def sum_a(zz, carry):
                    t = g32[n, x, zz, yy, :p, :]
                    for k in range(3):
                        t = t + ra[k, yy, zz].astype(F32)
                    ha[yy, zz] = t
                    ha16[yy, zz] = t.astype(BF16)
                    return carry
                lax.fori_loop(0, 4, sum_a, 0)
                if off:
                    middle[n][0].push(ha16.at[yy], r2a.at[off - 1], on_y(off))

        def part_c(i):
            if i < len(heavy[n][2]):
                heavy[n][2][i].arrive()
            slow = (planar(n, x, y)[0] + order[i]) % 4

            def sum_c(fast, carry):
                xs, yy = planar(n, slow, fast)
                t = g32[n, xs, zh, yy, pl.ds(pl.multiple_of(p + q + zl * 16, 8), 16), :]
                for k in range(7):
                    t = t + rc[k, slow, fast].astype(F32)
                hc[slow, fast] = t
                hc16[slow, fast] = t.astype(BF16)
                return carry
            lax.fori_loop(0, 4, sum_c, 0)
            if i < 3:
                middle[n][2].push(hc16.at[slow], r2c.at[order[i] - 1], on_slow[n](order[i]))

        for i in range(3):
            part_b(i)
        part_a()
        for i in range(3):
            part_c(i)
        part_b(3)
        part_c(3)

    last = [None, None]

    def second_sums(n):
        (ha, _), (hb, _), (hc, _), r2a, r2b, r2c, (js, jc), (r3, r3c) = lanes[n][9:17]
        js, js16 = js
        jc, jc16 = jc
        p, q, _ = CUTS[n]
        last[n] = [Group(r3), Group(r3c)]
        for group in middle[n]:
            group.arrive()

        def sum_ab(zz, carry):
            a, b = ha[y, zz], hb[x, zz]
            for k in range(3):
                a = a + r2a[k, zz].astype(F32)
                b = b + r2b[k, zz].astype(F32)
            for side in range(2):
                s, t = (p - 32) * side, (q - 32) * side
                v = jnp.concatenate([a[s:s + 32], b[t:t + 32]], axis=0)
                js[zz, side] = v
                js16[zz, side] = v.astype(BF16)
            return carry
        lax.fori_loop(0, 4, sum_ab, 0)
        for k in (4, 3, 5, 2, 6, 1, 7):
            there = (z + k) % 8
            last[n][0].push(js16.at[there // 2, there % 2], r3.at[k - 1], on_z(k))
        slow, fast = planar(n, x, y)
        for there in range(4):
            t = hc[slow, there]
            for k in range(3):
                t = t + r2c[k, there].astype(F32)
            jc[there] = t
            jc16[there] = t.astype(BF16)
        for k in (2, 1, 3):
            last[n][1].push(jc16.at[(fast + k) % 4], r3c.at[k - 1], on_fast[n](k))

    done = [None, None]

    def last_sums(n):
        (js, jc), (r3, r3c) = lanes[n][15:17]
        last[n][0].arrive()
        t = js[0][zh, zl]
        for k in range(7):
            t = t + r3[k].astype(F32)
        last[n][1].arrive()
        u = jc[0][planar(n, x, y)[1]]
        for k in range(3):
            u = u + r3c[k].astype(F32)
        fin[n, c * 2 + zl] = jnp.concatenate([t, u], axis=0)
        done[n] = spread_out(fin.at[0, three], fin.at[n, c * 2 + zl], (diagonal, partner, sibling))

    def finish(n):
        done[n].arrive()
        p, q, _ = CUTS[n]
        for core in range(2):
            lo, hi = fin[n, core * 2], fin[n, core * 2 + 1]
            v = jnp.concatenate([lo[0:32], hi[64 - p + 32 - 32:32], lo[32:64], hi[64 - q + 32:64],
                                 lo[64:80], hi[64:80]], axis=0)
            for half in range(2):
                begin = core * HALF + n * WIDE + half * 128
                cols = slice(begin, begin + 128)
                g = v[ROWS * half:ROWS * (half + 1)]
                grad_ref[:, cols] = g
                next_ref[:, cols] = (1.0 - ema_rate) * anchor_ref[:, cols] + ema_rate * (
                    policy_ref[:, cols] - step_size * g)

    second = second_start(0)
    started = third_start(0, second)
    second = second_start(1)
    rest0 = third_forward(0, started)
    started = third_start(1, second)
    own_x.wait()
    own_cot.wait()
    for group in sib:
        group.arrive()
    for group in rest0:
        group.arrive()
    first_product(0)
    make_signal(0)
    rest1 = third_forward(1, started)
    for i in range(4):
        second_product(0, i)
    for group in rest1:
        group.arrive()
    first_product(1)
    make_signal(1)
    for i in range(3):
        second_product(1, i)
    first_sums(0)
    second_product(1, 3)
    first_sums(1)
    second_sums(0)
    second_sums(1)
    last_sums(0)
    last_sums(1)
    finish(0)
    finish(1)

    for group in groups:
        group.sent()


def hand_over(a_in, b_in, a_out, b_out, held, sems):
    jobs = []
    for n, (src, dst) in enumerate(((a_in, a_out), (b_in, b_out))):
        jobs.append((pltpu.make_async_copy(src, held.at[n], sems.at[n]),
                     pltpu.make_async_copy(held.at[n], dst, sems.at[2 + n])))
    for fetch, _ in jobs:
        fetch.start()
    for fetch, store in jobs:
        fetch.wait()
        store.start()
    for _, store in jobs:
        store.wait()


def shards(inputs, cotangent, response_mask, policy, anchor):
    vmem = pl.BlockSpec(memory_space=pltpu.VMEM)
    hbm = pl.BlockSpec(memory_space=pl.ANY)
    scratch = [
        pltpu.VMEM((1, LEN), jnp.int32),
        pltpu.VMEM((ROWS, KVW), F32),
        pltpu.VMEM((ROWS, KVW), F32),
        pltpu.VMEM((2 * LEN, D), BF16),
        pltpu.VMEM((SLAB, WIDE), F32),
        pltpu.VMEM((D, WIDE), BF16),
        pltpu.VMEM((2 * LEN, WIDE), F32),
        pltpu.VMEM((2 * LEN, HALF), BF16),
        pltpu.VMEM((HALF, 2 * LEN), BF16),
        pltpu.VMEM((2, 8, LEN), F32),
        pltpu.VMEM((2, 4, 4, 4, PACK, 128), F32),
        pltpu.VMEM((2, 4, 80, 128), F32),
    ]
    for ag, (p, q, r) in zip(AG, CUTS):
        scratch += [pltpu.VMEM((4, 4, 4, m, 128), BF16) for m in ag]
        scratch += [pltpu.VMEM((4, 4, 4, m, 128), BF16) for m in (p, q, r)]
        scratch += [pltpu.VMEM((3, 4, 4, m, 128), BF16) for m in (p, q)]
        scratch += [pltpu.VMEM((7, 4, 4, 16, 128), BF16)]
        scratch += [(pltpu.VMEM((4, 4, m, 128), F32), pltpu.VMEM((4, 4, m, 128), BF16))
                    for m in (p, q, 16)]
        scratch += [pltpu.VMEM((3, 4, m, 128), BF16) for m in (p, q, 16)]
        scratch += [((pltpu.VMEM((4, 2, 64, 128), F32), pltpu.VMEM((4, 2, 64, 128), BF16)),
                     (pltpu.VMEM((4, 16, 128), F32), pltpu.VMEM((4, 16, 128), BF16)))]
        scratch += [(pltpu.VMEM((7, 64, 128), BF16), pltpu.VMEM((3, 16, 128), BF16))]
    scratch += [pltpu.SemaphoreType.DMA((NSEM,)), pltpu.SemaphoreType.DMA((NSEM,)),
                pltpu.SemaphoreType.DMA((5,))]
    rows = jax.ShapeDtypeStruct((ROWS, KVW), F32)
    sums = pl.pallas_call(
        kernel,
        out_shape=(rows, rows),
        in_specs=[hbm] * 5,
        out_specs=(vmem, vmem),
        scratch_shapes=scratch,
        compiler_params=pltpu.CompilerParams(
            collective_id=0, has_side_effects=True, vmem_limit_bytes=62 * 2**20),
        cost_estimate=pl.CostEstimate(flops=4 * LEN * D * KVW, bytes_accessed=20 * 2**20, transcendentals=0),
        name="policy_step",
    )(inputs, cotangent, response_mask, policy, anchor)
    return pl.pallas_call(
        hand_over,
        out_shape=(rows, rows),
        in_specs=[hbm, hbm],
        out_specs=(hbm, hbm),
        scratch_shapes=[pltpu.VMEM((2, ROWS, KVW), F32), pltpu.SemaphoreType.DMA((4,))],
        compiler_params=pltpu.CompilerParams(vmem_limit_bytes=62 * 2**20),
        name="hand_over",
    )(*sums)


def solution(mesh):
    placed = (
        P(("dp", "fsdp"), None, None),
        P(("dp", "fsdp"), None, None),
        P(("dp", "fsdp"), None),
        P("fsdp", None),
        P("fsdp", None),
    )
    return jax.shard_map(
        shards,
        mesh=mesh,
        in_specs=placed,
        out_specs=(P("fsdp", None), P("fsdp", None)),
        check_vma=False,
    )
```

```python
import jax
import jax.numpy as jnp
from jax import lax
from jax.experimental import pallas as pl
from jax.experimental.pallas import tpu as pltpu
from jax.sharding import PartitionSpec as P

kl_weight = 0.5
ema_rate = 0.01
step_size = 0.1

MESH = pl.DeviceIdType.MESH
F32 = jnp.float32
BF16 = jnp.bfloat16

LEN = 768
D = 4608
KVW = 1024
HALF = KVW // 2
WIDE = HALF // 2
ROWS = 72
SLAB = 16 * ROWS
PACK = 2 * ROWS
CUTS = ((64, 48, 32), (48, 64, 32))
AG = ((64, 64, 16), (64, 64, 16))
NSEM = 64


def kernel(x_hbm, cot_hbm, mask_hbm, policy_hbm, anchor_hbm, grad_ref,
           mask_ref, policy_ref, anchor_ref, xv, stage, dcol, spread, cot, sig_t, scale, g32, fin, *rest):
    lanes = [rest[17 * i:17 * (i + 1)] for i in range(2)]
    ssem, rsem, loc = rest[34:]
    dp, fs = lax.axis_index("dp"), lax.axis_index("fsdp")
    c, zl = dp % 2, dp // 2
    x, zh, y = fs // 16, (fs // 4) % 4, fs % 4
    z = zh * 2 + zl

    def at(c_, x_, y_, z_):
        return ((z_ % 2) * 2 + c_, (x_ * 4 + z_ // 2) * 4 + y_)

    def on_x(k):
        return at(c, (x + k) % 4, y, z)

    def on_y(k):
        return at(c, x, (y + k) % 4, z)

    def on_z(k):
        return at(c, x, y, (z + k) % 8)

    def on_pairs(k):
        return on_z(jnp.where(zl == 1, k, 8 - k))

    sibling = at(1 - c, x, y, z)
    partner = at(c, x, y, zh * 2 + (1 - zl))
    diagonal = at(1 - c, x, y, zh * 2 + (1 - zl))

    groups = []

    class Group:
        def __init__(self, span):
            self.span, self.n = span, len(groups)
            groups.append(self)

        def push(self, src, dst, device):
            pltpu.make_async_remote_copy(
                src_ref=src, dst_ref=dst, send_sem=ssem.at[self.n], recv_sem=rsem.at[self.n],
                device_id=device, device_id_type=MESH).start()

        def arrive(self):
            pltpu.make_async_copy(self.span, self.span, rsem.at[self.n]).wait()

        def sent(self):
            pltpu.make_async_copy(self.span, self.span, ssem.at[self.n]).wait()

    def spread_out(span, ref, targets):
        group = Group(span)
        for device in targets:
            group.push(ref, ref, device)
        return group

    def planar(n, xs, yy):
        return (xs, yy) if n else (yy, xs)

    on_slow, on_fast = (on_y, on_x), (on_x, on_y)

    small = [pltpu.make_async_copy(src, dst, loc.at[2 + n]) for n, (src, dst) in enumerate((
        (policy_hbm, policy_ref), (anchor_hbm, anchor_ref), (mask_hbm, mask_ref)))]
    for copy in small:
        copy.start()
    own_x = pltpu.make_async_copy(x_hbm.at[0], xv.at[pl.ds(0, LEN)], loc.at[0])
    own_x.start()
    mine = pl.multiple_of(c * HALF, HALF)
    other = pl.multiple_of((1 - c) * HALF, HALF)
    own_cot = pltpu.make_async_copy(
        cot_hbm.at[0, :, pl.ds(mine, HALF)], cot.at[pl.ds(0, LEN)], loc.at[1])
    own_cot.start()

    barrier = pltpu.get_barrier_semaphore()
    peers = [on_x(k) for k in (1, 2, 3)] + [on_y(k) for k in (1, 2, 3)]
    peers += [on_z(k) for k in range(1, 8)] + [sibling, diagonal]
    for device in peers:
        pl.semaphore_signal(barrier, inc=1, device_id=device, device_id_type=MESH)

    for copy in small:
        copy.wait()
    delta = policy_ref[...] - anchor_ref[...]
    delta = jnp.where(c == 0, delta[:, :HALF], delta[:, HALF:])
    for n, (ta, tb, tc, *_) in enumerate(lanes):
        p, q, _ = AG[n]
        v = jnp.concatenate([delta[:, WIDE * n:WIDE * n + 128], delta[:, WIDE * n + 128:WIDE * n + 256]], axis=0)
        ta[x, y, zh] = v[:p].astype(BF16)
        tb[y, x, zh] = v[p:p + q].astype(BF16)
        tc[(zh, *planar(n, x, y))] = v[p + q:].astype(BF16)
    weights = mask_ref[...].astype(F32)
    weights = weights / jnp.sum(weights, axis=1, keepdims=True)
    scale[0] = jnp.broadcast_to(weights, (8, LEN))

    pl.semaphore_wait(barrier, len(peers))

    three = pl.ds(0, 3)
    first = []
    for n, (ta, tb, tc, *_) in enumerate(lanes):
        first.append([
            spread_out(ta.at[0, 0, three], ta.at[x, y, zh], [on_pairs(k) for k in (1, 2, 3)]),
            spread_out(tb.at[0, 0, three], tb.at[y, x, zh], [on_pairs(k) for k in (1, 2, 3)]),
            spread_out(tc.at[0, 0, three], tc.at[(zh, *planar(n, x, y))],
                       [on_fast[n](k) for k in (1, 2, 3)])])

    sib = [Group(xv.at[pl.ds(LEN, LEN)]), Group(cot.at[pl.ds(LEN, LEN)]), Group(scale.at[1])]
    sib[0].push(x_hbm.at[0], xv.at[pl.ds(LEN, LEN)], sibling)
    sib[1].push(cot_hbm.at[0, :, pl.ds(other, HALF)], cot.at[pl.ds(LEN, LEN)], sibling)
    sib[2].push(scale.at[0], scale.at[1], sibling)

    def second_start(n):
        ta, tb, tc = lanes[n][:3]
        first[n][0].arrive()
        pa = spread_out(ta.at[0, three], ta.at[x, y], [on_y(k) for k in (1, 2, 3)])
        first[n][1].arrive()
        pb = spread_out(tb.at[0, three], tb.at[y, x], [on_x(k) for k in (1, 2, 3)])
        first[n][2].arrive()
        pc = spread_out(tc.at[0, three], tc.at[zh, planar(n, x, y)[0]], [on_slow[n](k) for k in (1, 2, 3)])
        return pa, pb, pc

    front, back = pl.ds(0, 2), pl.ds(2, 2)

    def ring_start(t, me, on):
        one, two = Group(t.at[0]), Group(t.at[0])
        for group, rows, k in ((one, front, 1), (one, back, 3), (two, back, 1), (two, front, 3)):
            group.push(t.at[me, rows], t.at[me, rows], on(k))
        return one, two

    def ring_forward(t, me, on, started):
        started[0].arrive()
        group = Group(t.at[0])
        for owner, rows, k in (((me + 3) % 4, front, 1), ((me + 1) % 4, back, 3)):
            group.push(t.at[owner, rows], t.at[owner, rows], on(k))
        return started[1], group

    def third_start(n, second):
        ta, tb, tc = lanes[n][:3]
        second[0].arrive()
        a = ring_start(ta, x, on_x)
        second[1].arrive()
        b = ring_start(tb, y, on_y)
        second[2].arrive()
        c1 = [spread_out(tc.at[0, half], tc.at[zh, half], [on_pairs(1)]) for half in (front, back)]
        return a, b, c1

    def third_forward(n, started):
        ta, tb, tc = lanes[n][:3]
        a, b, c1 = started
        a = ring_forward(ta, x, on_x, a)
        b = ring_forward(tb, y, on_y, b)
        relay = Group(tc.at[pl.ds(0, 2)])
        owner = (zh + jnp.where(zl == 1, 1, 3)) % 4
        for group, half in zip(c1, (front, back)):
            group.arrive()
            for k in (1, 2):
                relay.push(tc.at[owner, half], tc.at[owner, half], on_z(jnp.where(zl == 1, 8 - k, k)))
        return (*a, *b, relay)

    def first_product(n):
        ta, tb, tc = lanes[n][:3]
        for xs in range(4):
            def unpack(i, carry):
                yy, zz = i // 4, i % 4
                v = jnp.concatenate([ta[xs, yy, zz].astype(F32), tb[yy, xs, zz].astype(F32),
                                     tc[(zz, *planar(n, xs, yy))].astype(F32)], axis=0)
                row = pl.ds(pl.multiple_of(zz * 288 + yy * ROWS, 8), ROWS)
                stage[row, 0:128] = v[:ROWS]
                stage[row, 128:256] = v[ROWS:]
                return carry
            lax.fori_loop(0, 16, unpack, 0)
            dcol[SLAB * xs:SLAB * (xs + 1), :] = stage[...].astype(BF16)

        def tokens(m):
            rows = pl.ds(m * LEN, LEN)
            spread[rows, :] = jnp.dot(xv[rows, :], dcol[...], preferred_element_type=F32)
        tokens(0)
        tokens(1)

    def make_signal(n):
        cols = slice(WIDE * n, WIDE * (n + 1))

        def tokens(m, carry):
            rows = pl.ds(pl.multiple_of(m * 256, 256), 256)
            u = cot[rows, cols].astype(F32) + kl_weight * spread[rows, :]
            lane = pl.ds(pl.multiple_of((m % 3) * 256, 256), 256)
            w = scale[m // 3, 0:1, lane]
            sig_t[cols, rows] = (u.T * w).astype(BF16)
            return carry
        lax.fori_loop(0, 6, tokens, 0)

    near = jnp.where(x % 2 == 0, 1, 3)
    order = (2, 4 - near, near, 0)
    heavy = [[None, [], None], [None, [], None]]

    def second_product(n, i):
        ga, gb, gc, ra, rb, rc = lanes[n][3:9]
        p, q, _ = CUTS[n]
        off = order[i]
        xs = (x + off) % 4
        out = jnp.dot(sig_t[WIDE * n:WIDE * (n + 1), :], xv[:, pl.ds(pl.multiple_of(xs * SLAB, 128), SLAB)],
                      preferred_element_type=F32)
        stage[...] = out.T

        def pack(m, carry):
            yy, zz = m // 4, m % 4
            row = pl.ds(pl.multiple_of(zz * 288 + yy * ROWS, 8), ROWS)
            v = jnp.concatenate([stage[row, 0:128], stage[row, 128:256]], axis=0)
            g32[n, xs, zz, yy] = v
            ga[xs, yy, zz] = v[:p].astype(BF16)
            gb[yy, xs, zz] = v[p:p + q].astype(BF16)
            gc[(zz, *planar(n, xs, yy))] = v[p + q:].astype(BF16)
            return carry
        lax.fori_loop(0, 16, pack, 0)
        if i == 0:
            heavy[n][0], heavy[n][2] = Group(ra), [] if n else [Group(rc)]
        if i < 3:
            heavy[n][0].push(ga.at[xs], ra.at[off - 1], on_x(off))
        heavy[n][1].append(Group(rb.at[:, 0]))
        for k in (2, 1, 3):
            heavy[n][1][i].push(gb.at[(y + k) % 4, xs], rb.at[k - 1, xs], on_y(k))
        if n:
            heavy[n][2].append(Group(rc.at[:, 0]))
        for k in (4, 3, 5, 2, 6, 1, 7):
            there = (z + k) % 8
            window = pl.ds(pl.multiple_of((there % 2) * 16, 16), 16)
            if n:
                heavy[n][2][i].push(gc.at[there // 2, xs, :, window], rc.at[k - 1, xs], on_z(k))
            else:
                heavy[n][2][0].push(gc.at[there // 2, :, xs, window], rc.at[k - 1, :, xs], on_z(k))

    middle = [None, None]

    def first_sums(n):
        ra, rb, rc, ha, hb, hc, r2a, r2b, r2c = lanes[n][6:15]
        ha, ha16 = ha
        hb, hb16 = hb
        hc, hc16 = hc
        p, q, _ = CUTS[n]
        middle[n] = [Group(r2a), Group(r2b), Group(r2c)]

        def part_b(i):
            xs = (x + order[i]) % 4
            heavy[n][1][i].arrive()

            def sum_b(zz, carry):
                t = g32[n, xs, zz, y, p:p + q, :]
                for k in range(3):
                    t = t + rb[k, xs, zz].astype(F32)
                hb[xs, zz] = t
                hb16[xs, zz] = t.astype(BF16)
                return carry
            lax.fori_loop(0, 4, sum_b, 0)
            if i < 3:
                middle[n][1].push(hb16.at[xs], r2b.at[order[i] - 1], on_x(order[i]))

        def part_a():
            heavy[n][0].arrive()
            for off in (2, 1, 3, 0):
                yy = (y + off) % 4

                def sum_a(zz, carry):
                    t = g32[n, x, zz, yy, :p, :]
                    for k in range(3):
                        t = t + ra[k, yy, zz].astype(F32)
                    ha[yy, zz] = t
                    ha16[yy, zz] = t.astype(BF16)
                    return carry
                lax.fori_loop(0, 4, sum_a, 0)
                if off:
                    middle[n][0].push(ha16.at[yy], r2a.at[off - 1], on_y(off))

        def part_c(i):
            if i < len(heavy[n][2]):
                heavy[n][2][i].arrive()
            slow = (planar(n, x, y)[0] + order[i]) % 4

            def sum_c(fast, carry):
                xs, yy = planar(n, slow, fast)
                t = g32[n, xs, zh, yy, pl.ds(pl.multiple_of(p + q + zl * 16, 8), 16), :]
                for k in range(7):
                    t = t + rc[k, slow, fast].astype(F32)
                hc[slow, fast] = t
                hc16[slow, fast] = t.astype(BF16)
                return carry
            lax.fori_loop(0, 4, sum_c, 0)
            if i < 3:
                middle[n][2].push(hc16.at[slow], r2c.at[order[i] - 1], on_slow[n](order[i]))

        for i in range(3):
            part_b(i)
        part_a()
        for i in range(3):
            part_c(i)
        part_b(3)
        part_c(3)

    last = [None, None]

    def second_sums(n):
        (ha, _), (hb, _), (hc, _), r2a, r2b, r2c, (js, jc), (r3, r3c) = lanes[n][9:17]
        js, js16 = js
        jc, jc16 = jc
        p, q, _ = CUTS[n]
        last[n] = [Group(r3), Group(r3c)]
        for group in middle[n]:
            group.arrive()

        def sum_ab(zz, carry):
            a, b = ha[y, zz], hb[x, zz]
            for k in range(3):
                a = a + r2a[k, zz].astype(F32)
                b = b + r2b[k, zz].astype(F32)
            for side in range(2):
                s, t = (p - 32) * side, (q - 32) * side
                v = jnp.concatenate([a[s:s + 32], b[t:t + 32]], axis=0)
                js[zz, side] = v
                js16[zz, side] = v.astype(BF16)
            return carry
        lax.fori_loop(0, 4, sum_ab, 0)
        for k in (4, 3, 5, 2, 6, 1, 7):
            there = (z + k) % 8
            last[n][0].push(js16.at[there // 2, there % 2], r3.at[k - 1], on_z(k))
        slow, fast = planar(n, x, y)
        for there in range(4):
            t = hc[slow, there]
            for k in range(3):
                t = t + r2c[k, there].astype(F32)
            jc[there] = t
            jc16[there] = t.astype(BF16)
        for k in (2, 1, 3):
            last[n][1].push(jc16.at[(fast + k) % 4], r3c.at[k - 1], on_fast[n](k))

    done = [None, None]

    def last_sums(n):
        (js, jc), (r3, r3c) = lanes[n][15:17]
        last[n][0].arrive()
        t = js[0][zh, zl]
        for k in range(7):
            t = t + r3[k].astype(F32)
        last[n][1].arrive()
        u = jc[0][planar(n, x, y)[1]]
        for k in range(3):
            u = u + r3c[k].astype(F32)
        fin[n, c * 2 + zl] = jnp.concatenate([t, u], axis=0)
        done[n] = spread_out(fin.at[0, three], fin.at[n, c * 2 + zl], (diagonal, partner, sibling))

    def finish(n):
        done[n].arrive()
        p, q, _ = CUTS[n]
        for core in range(2):
            lo, hi = fin[n, core * 2], fin[n, core * 2 + 1]
            v = jnp.concatenate([lo[0:32], hi[64 - p + 32 - 32:32], lo[32:64], hi[64 - q + 32:64],
                                 lo[64:80], hi[64:80]], axis=0)
            for half in range(2):
                begin = core * HALF + n * WIDE + half * 128
                cols = slice(begin, begin + 128)
                grad_ref[:, cols] = v[ROWS * half:ROWS * (half + 1)]

    second = second_start(0)
    started = third_start(0, second)
    second = second_start(1)
    rest0 = third_forward(0, started)
    started = third_start(1, second)
    own_x.wait()
    own_cot.wait()
    for group in sib:
        group.arrive()
    for group in rest0:
        group.arrive()
    first_product(0)
    rest1 = third_forward(1, started)
    make_signal(0)
    for i in range(4):
        second_product(0, i)
    for group in rest1:
        group.arrive()
    first_product(1)
    make_signal(1)
    for i in range(3):
        second_product(1, i)
    first_sums(0)
    second_product(1, 3)
    first_sums(1)
    second_sums(0)
    second_sums(1)
    last_sums(0)
    last_sums(1)
    finish(0)
    finish(1)

    for group in groups:
        group.sent()


def hand_over(sum_in, policy_in, anchor_in, grad_out, next_out, held, sems):
    fetches = [pltpu.make_async_copy(src, held.at[n], sems.at[n])
               for n, src in enumerate((sum_in, policy_in, anchor_in))]
    for fetch in fetches:
        fetch.start()
    fetches[0].wait()
    stores = [pltpu.make_async_copy(held.at[0], grad_out, sems.at[3]),
              pltpu.make_async_copy(held.at[3], next_out, sems.at[4])]
    stores[0].start()
    fetches[1].wait()
    fetches[2].wait()
    held[3] = (1.0 - ema_rate) * held[2] + ema_rate * (held[1] - step_size * held[0])
    stores[1].start()
    for store in stores:
        store.wait()


def shards(inputs, cotangent, response_mask, policy, anchor):
    vmem = pl.BlockSpec(memory_space=pltpu.VMEM)
    hbm = pl.BlockSpec(memory_space=pl.ANY)
    scratch = [
        pltpu.VMEM((1, LEN), jnp.int32),
        pltpu.VMEM((ROWS, KVW), F32),
        pltpu.VMEM((ROWS, KVW), F32),
        pltpu.VMEM((2 * LEN, D), BF16),
        pltpu.VMEM((SLAB, WIDE), F32),
        pltpu.VMEM((D, WIDE), BF16),
        pltpu.VMEM((2 * LEN, WIDE), F32),
        pltpu.VMEM((2 * LEN, HALF), BF16),
        pltpu.VMEM((HALF, 2 * LEN), BF16),
        pltpu.VMEM((2, 8, LEN), F32),
        pltpu.VMEM((2, 4, 4, 4, PACK, 128), F32),
        pltpu.VMEM((2, 4, 80, 128), F32),
    ]
    for ag, (p, q, r) in zip(AG, CUTS):
        scratch += [pltpu.VMEM((4, 4, 4, m, 128), BF16) for m in ag]
        scratch += [pltpu.VMEM((4, 4, 4, m, 128), BF16) for m in (p, q, r)]
        scratch += [pltpu.VMEM((3, 4, 4, m, 128), BF16) for m in (p, q)]
        scratch += [pltpu.VMEM((7, 4, 4, 16, 128), BF16)]
        scratch += [(pltpu.VMEM((4, 4, m, 128), F32), pltpu.VMEM((4, 4, m, 128), BF16))
                    for m in (p, q, 16)]
        scratch += [pltpu.VMEM((3, 4, m, 128), BF16) for m in (p, q, 16)]
        scratch += [((pltpu.VMEM((4, 2, 64, 128), F32), pltpu.VMEM((4, 2, 64, 128), BF16)),
                     (pltpu.VMEM((4, 16, 128), F32), pltpu.VMEM((4, 16, 128), BF16)))]
        scratch += [(pltpu.VMEM((7, 64, 128), BF16), pltpu.VMEM((3, 16, 128), BF16))]
    scratch += [pltpu.SemaphoreType.DMA((NSEM,)), pltpu.SemaphoreType.DMA((NSEM,)),
                pltpu.SemaphoreType.DMA((5,))]
    rows = jax.ShapeDtypeStruct((ROWS, KVW), F32)
    total = pl.pallas_call(
        kernel,
        out_shape=rows,
        in_specs=[hbm] * 5,
        out_specs=vmem,
        scratch_shapes=scratch,
        compiler_params=pltpu.CompilerParams(
            collective_id=0, has_side_effects=True, vmem_limit_bytes=62 * 2**20),
        cost_estimate=pl.CostEstimate(flops=4 * LEN * D * KVW, bytes_accessed=20 * 2**20, transcendentals=0),
        name="policy_step",
    )(inputs, cotangent, response_mask, policy, anchor)
    return pl.pallas_call(
        hand_over,
        out_shape=(rows, rows),
        in_specs=[hbm] * 3,
        out_specs=(hbm, hbm),
        scratch_shapes=[pltpu.VMEM((4, ROWS, KVW), F32), pltpu.SemaphoreType.DMA((5,))],
        compiler_params=pltpu.CompilerParams(vmem_limit_bytes=62 * 2**20),
        name="hand_over",
    )(total, policy, anchor)


def solution(mesh):
    placed = (
        P(("dp", "fsdp"), None, None),
        P(("dp", "fsdp"), None, None),
        P(("dp", "fsdp"), None),
        P("fsdp", None),
        P("fsdp", None),
    )
    return jax.shard_map(
        shards,
        mesh=mesh,
        in_specs=placed,
        out_specs=(P("fsdp", None), P("fsdp", None)),
        check_vma=False,
    )
```
